512 devices in a mesh: chan: 64 (over y_lo, z, x), freq: 8 (over y_hi, core).
Axes of the slice: x: 4, y: 8 (y_hi: 4, y_lo: 2; y = y_hi * 2 + y_lo), z: 8, core: 2. Of those that a mesh axis runs over, the one named last changes fastest.
Arguments:
- spectra: bfloat16 [20480, 2, 2, 2048], P('chan', None, None, 'freq'), may hold values from -60 to 60
- validity: int32 [20480, 2], P('chan'), may hold values from 0 to 1, as said below
- pair_mask: int32 [64, 2, 5, 5], replicated, may hold values from 0 to 1, as said below
- owners: int32 [64, 50], replicated, may hold values from 0 to 63, as said below
Outputs:
- stacked: bfloat16 [64, 64, 1, 64, 256], P('chan', None, None, 'freq')
The draws below stay inside these ranges and needn't reach their ends.
Inputs may be any that keep to these rules, and one draw needn't show every extreme that they name: `validity`: some channels have no usable segment. `pair_mask`: entry [b, d, u, v] pairs sub-block u of block b with sub-block v of block (b + d + 1) mod 64. Each block lists the distances 1 up to a level of its own, at least distance 1; some block lists all 2. A row gives the owners of one block's candidate sub-tiles in order, in runs of 1 consecutive entries; the runs of a row go to distinct owners, so one owner gets at most 1 of one block's sub-tiles, and the first run reaches it.
All inputs are finite; a program needn't handle non-finite values.
Results may differ from the reference program's by a relative error of at most 0.02.
Values may be sent and summed in bfloat16 or wider, within the bound.
No kernel may reach another device: no remote copies, remote signals or barrier semaphores. Data moves between devices by JAX's collectives and lax.ppermute only.
A program may use at most 64 MiB of HBM per device.

```python
import math
import jax
import jax.numpy as jnp
from jax import lax

CH_DEV = 320
SB = 64
FREQS = 2048
SEG = 2
LAGS = 4
LAG_STEP = 25
HALF = 32
REACH = 2
BLOCKS = 64
CHANNELS = 20480
SUB = 5
CAPS = 1
N_FREQ = 8


def draw_spectra(key, part):
    key = jax.random.fold_in(key, 11)
    key_one, key_two, key_three = jax.random.split(key, 3)
    base_draw = jnp.clip(jax.random.normal(key_one, (CHANNELS, 2, SEG, FREQS), jnp.float32), -6.0, 6.0)
    log_span = math.log(10.0)
    chan_scale = jnp.exp(jax.random.uniform(key_two, (CHANNELS, 1, 1, 1), jnp.float32, 0.0, log_span))
    bin_scale = jnp.exp(jax.random.uniform(key_three, (CHANNELS, 1, 1, FREQS), jnp.float32, 0.0, log_span))
    return (base_draw * chan_scale * bin_scale * 0.1).astype(jnp.bfloat16)


def draw_validity(key, part):
    key = jax.random.fold_in(key, 12)
    key_one, key_two, key_three = jax.random.split(key, 3)
    dead_channel = jax.random.randint(key_one, (CHANNELS, 1), 0, 16) == 0
    forced = jnp.arange(CHANNELS, dtype=jnp.int32)[:, None] == jax.random.randint(key_three, (), 0, CHANNELS)
    usable = jax.random.randint(key_two, (CHANNELS, SEG), 0, 4) < 3
    return jnp.where(dead_channel | forced, 0, usable.astype(jnp.int32)).astype(jnp.int32)


def draw_pair_mask(key, part):
    key = jax.random.fold_in(key, 13)
    key_one, key_two, key_three = jax.random.split(key, 3)
    pair_level = jax.random.randint(key_one, (BLOCKS,), 1, REACH + 1)
    forced = jnp.arange(BLOCKS, dtype=jnp.int32) == jax.random.randint(key_three, (), 0, BLOCKS)
    pair_level = jnp.where(forced, REACH, pair_level)
    distance = jnp.arange(1, REACH + 1, dtype=jnp.int32)
    active = distance[None, :] <= pair_level[:, None]
    listed = jax.random.randint(key_two, (BLOCKS, REACH, SUB, SUB), 0, 3) < 2
    return (active[:, :, None, None] & listed).astype(jnp.int32)


def draw_owners(key, part):
    key = jax.random.fold_in(key, 14)
    row_keys = jax.random.split(key, BLOCKS)
    orders = jax.vmap(lambda row_key: jax.random.permutation(row_key, BLOCKS))(row_keys)
    run_index = jnp.arange(REACH * SUB * SUB, dtype=jnp.int32) // CAPS
    return orders[:, run_index].astype(jnp.int32)


def setup_inputs(seed: int = 0) -> dict:
    arg_keys = jax.random.split(jax.random.key(seed), 5)
    return {
        "spectra": draw_spectra(jax.random.fold_in(arg_keys[4], 71), 0),
        "validity": draw_validity(jax.random.fold_in(arg_keys[4], 71), 0),
        "pair_mask": draw_pair_mask(jax.random.fold_in(arg_keys[4], 71), 0),
        "owners": draw_owners(jax.random.fold_in(arg_keys[4], 71), 0),
    }


EPS = 1e-06

def lag_tables(first_bin, count):
    bin_index = first_bin + jnp.arange(count, dtype=jnp.int32)
    lag_values = (jnp.arange(LAGS, dtype=jnp.int32) - LAGS // 2) * LAG_STEP
    turn_count = lag_values[:, None] * bin_index[None, :] % (2 * FREQS)
    phase_angle = turn_count.astype(jnp.float32) * (math.pi / FREQS)
    return (jnp.cos(phase_angle), jnp.sin(phase_angle))

def amplitude_sum(values, weights):
    magnitude = jnp.sqrt(values[:, 0] ** 2 + values[:, 1] ** 2)
    return lax.optimization_barrier(jnp.sum(magnitude * weights[:, :, None], axis=1))

def whiten(values, weights, padded, first_bin, count):
    cumulate = jnp.cumsum(padded, axis=1)
    cumulate = jnp.concatenate([jnp.zeros((padded.shape[0], 1), jnp.float32), cumulate], axis=1)
    window = cumulate[:, 2 * HALF + 1:] - cumulate[:, :count]
    bin_index = first_bin + jnp.arange(count, dtype=jnp.int32)
    lower = jnp.maximum(bin_index - HALF, 0)
    upper = jnp.minimum(bin_index + HALF, FREQS - 1)
    bin_count = (upper - lower + 1).astype(jnp.float32)
    seg_count = jnp.maximum(lax.optimization_barrier(jnp.sum(weights, axis=1)), 1.0)
    mean_level = window / (bin_count[None, :] * seg_count[:, None])
    scaled = values * weights[:, None, :, None] / (mean_level[:, None, None, :] + EPS)
    return scaled.astype(jnp.bfloat16)

def rotate(right_block, cosine_table, sine_table):
    right_float = right_block.astype(jnp.float32)
    real_part = right_float[None, :, 0] * cosine_table[:, None, None, :] + right_float[None, :, 1] * sine_table[:, None, None, :]
    imag_part = right_float[None, :, 1] * cosine_table[:, None, None, :] - right_float[None, :, 0] * sine_table[:, None, None, :]
    return jnp.stack([real_part, imag_part], axis=2).astype(jnp.bfloat16)

def block_tile(left_block, right_block, left_valid, right_valid):
    cosine_table, sine_table = lag_tables(0, FREQS)
    rotated = rotate(right_block, cosine_table, sine_table)
    group_size = FREQS // N_FREQ
    left_group = left_block.astype(jnp.float32).reshape(CH_DEV, 2, SEG, N_FREQ, group_size)
    right_group = rotated.astype(jnp.float32).reshape(LAGS, CH_DEV, 2, SEG, N_FREQ, group_size)
    partial_value = jnp.einsum('ipsgf,ljpsgf->gilj', left_group, right_group)
    rounded = lax.optimization_barrier(partial_value.astype(jnp.bfloat16))
    summed = lax.optimization_barrier(jnp.sum(rounded.astype(jnp.float32), axis=0))
    joint_count = jnp.dot(left_valid.astype(jnp.float32), right_valid.astype(jnp.float32).T, precision=lax.Precision.HIGHEST)
    scaling = 1.0 / jnp.sqrt(jnp.maximum(joint_count, 1.0) * FREQS)
    correlated = (summed * scaling[:, None, :]).astype(jnp.bfloat16)
    pieces = correlated.reshape(SUB, SB, LAGS, SUB, SB).transpose(0, 3, 1, 2, 4)
    return pieces.reshape(SUB * SUB, SB, LAGS * SB)

def block_pieces(block_id, whitened, valid_in, pair_mask):
    left_block = lax.dynamic_index_in_dim(whitened, block_id, 0, keepdims=False)
    left_valid = lax.dynamic_index_in_dim(valid_in, block_id, 0, keepdims=False)
    mask_row = lax.dynamic_index_in_dim(pair_mask, block_id, 0, keepdims=False)
    collected = []
    for distance in range(1, REACH + 1):
        other_id = ((block_id + distance) % BLOCKS).astype(jnp.int32)
        right_block = lax.dynamic_index_in_dim(whitened, other_id, 0, keepdims=False)
        right_valid = lax.dynamic_index_in_dim(valid_in, other_id, 0, keepdims=False)
        listed = mask_row[distance - 1].reshape(SUB * SUB)
        pieces = lax.cond(jnp.sum(listed) > 0, lambda: block_tile(left_block, right_block, left_valid, right_valid), lambda: jnp.zeros((SUB * SUB, SB, LAGS * SB), jnp.bfloat16))
        collected.append(pieces * listed.astype(jnp.bfloat16)[:, None, None])
    return jnp.concatenate(collected, axis=0)

def reference(spectra, validity, pair_mask, owners):
    blocks_in = spectra.reshape(BLOCKS, CH_DEV, 2, SEG, FREQS)
    valid_in = validity.reshape(BLOCKS, CH_DEV, SEG)

    def whiten_one(inputs):
        block_data, valid_block = inputs
        values = block_data.astype(jnp.float32)
        weights = valid_block.astype(jnp.float32)
        padded = jnp.pad(amplitude_sum(values, weights), ((0, 0), (HALF, HALF)))
        return whiten(values, weights, padded, 0, FREQS)
    whitened = lax.map(whiten_one, (blocks_in, valid_in))

    def pieces_of(block_id):
        return block_pieces(block_id, whitened, valid_in, pair_mask)
    pieces = lax.map(pieces_of, jnp.arange(BLOCKS, dtype=jnp.int32))
    source = jnp.broadcast_to(jnp.arange(BLOCKS, dtype=jnp.int32)[:, None], owners.shape)
    slot_grid = jnp.broadcast_to(jnp.arange(owners.shape[1], dtype=jnp.int32)[None, :] % CAPS, owners.shape)
    stacked = jnp.zeros((BLOCKS, BLOCKS, CAPS, SB, LAGS * SB), jnp.bfloat16)
    return stacked.at[owners, source, slot_grid].set(pieces)
```

```python
import functools

import jax
import jax.numpy as jnp
import numpy as np
from jax import lax
from jax.experimental import pallas as pl
from jax.experimental.pallas import tpu as pltpu
from jax.sharding import PartitionSpec as P

FREQS = 2048
LAGS = 4
LAG_STEP = 25
HALF = 32
EPS = 1e-06

SUB = 5
SB = 64
CH = 320
BAND = 256
PARTS = 4
REACH = 2
N_FREQ = 8
BLOCKS = 64
SHARE = SB // N_FREQ
ROWS = REACH * SUB * SHARE
COLS = SUB * LAGS * SB
VALID_LANE = 2 * HALF
MIB = 1 << 20

VMEM = pl.BlockSpec(memory_space=pltpu.VMEM)
SMEM = pl.BlockSpec(memory_space=pltpu.SMEM)


def bin_tables():
    bins = np.arange(FREQS)
    lags = (np.arange(LAGS) - LAGS // 2) * LAG_STEP
    angle = np.pi * ((lags[:, None] * bins[None, :]) % (2 * FREQS)) / FREQS
    count = np.minimum(bins + HALF, FREQS - 1) - np.maximum(bins - HALF, 0) + 1
    rows = np.concatenate([np.cos(angle), np.sin(angle), np.tile(count, (8, 1))])
    return np.ascontiguousarray(
        rows.reshape(16, N_FREQ, BAND).transpose(1, 0, 2).astype(np.float32)
    )


def window_tables():
    out_bin = np.arange(BAND)[None, :]
    inner = np.abs(np.arange(BAND)[:, None] - out_bin) <= HALF
    low = np.abs(np.arange(-HALF, 0)[:, None] - out_bin) <= HALF
    high = np.abs(np.arange(BAND, BAND + HALF)[:, None] - out_bin) <= HALF
    message = np.zeros((128, 3 * BAND))
    message[:HALF, :BAND] = low
    message[HALF : 2 * HALF, :BAND] = high
    message[VALID_LANE, BAND : 2 * BAND] = 1
    message[VALID_LANE + 1, 2 * BAND :] = 1
    return inner.astype(jnp.bfloat16), message.astype(jnp.bfloat16)


def part(ref, rows, index):
    return ref[rows, index * BAND : (index + 1) * BAND].astype(jnp.float32)


def amplitude(ref, rows, weight_one, weight_two):
    first = jnp.sqrt(part(ref, rows, 0) ** 2 + part(ref, rows, 2) ** 2)
    second = jnp.sqrt(part(ref, rows, 1) ** 2 + part(ref, rows, 3) ** 2)
    return first * weight_one + second * weight_two


def edges_kernel(raw, valid, low, high):
    for start in range(0, CH, SB):
        rows = slice(start, start + SB)
        weight = valid[rows, :].astype(jnp.float32)
        level = amplitude(raw, rows, weight[:, 0:1], weight[:, 1:2]).astype(jnp.bfloat16)
        low[rows, :] = level[:, :HALF]
        high[rows, :] = level[:, BAND - HALF :]


def tiles_kernel(
    odd, here, before, after, note_here, note_before, note_after, table, inner, spread,
    mine, theirs, level, gains, left, right,
):
    def prepare(raw, note):
        wide = jnp.dot(note[...], spread[...], preferred_element_type=jnp.float32)
        gains[...] = wide
        for start in range(0, CH, SB):
            rows = slice(start, start + SB)
            level[rows, :] = amplitude(
                raw, rows, gains[rows, BAND : 2 * BAND], gains[rows, 2 * BAND :]
            ).astype(jnp.bfloat16)
        gains[:, :BAND] += jnp.dot(
            level[...], inner[...], preferred_element_type=jnp.float32
        )

    def whitened(raw, rows):
        one, two = gains[rows, BAND : 2 * BAND], gains[rows, 2 * BAND :]
        mean = gains[rows, :BAND] / (table[8:9, :] * jnp.maximum(one + two, 1.0))
        scale = 1.0 / (mean + EPS)
        one, two = one * scale, two * scale
        return [part(raw, rows, i) * (two if i % 2 else one) for i in range(PARTS)]

    prepare(after, note_after)
    for u in range(SUB):
        rows = slice(u * SB, (u + 1) * SB)
        white = [x.astype(jnp.bfloat16) for x in whitened(after, rows)]
        for lag in range(LAGS):
            dest = slice(u * LAGS * SB + lag * SB, u * LAGS * SB + (lag + 1) * SB)
            for s in range(2):
                real, imag = white[s], white[2 + s]
                if lag != LAGS // 2:
                    cosine, sine = table[lag : lag + 1, :], table[4 + lag : 5 + lag, :]
                    real, imag = real.astype(jnp.float32), imag.astype(jnp.float32)
                    real, imag = (
                        (real * cosine + imag * sine).astype(jnp.bfloat16),
                        (imag * cosine - real * sine).astype(jnp.bfloat16),
                    )
                right[dest, s * BAND : (s + 1) * BAND] = real
                right[dest, (2 + s) * BAND : (3 + s) * BAND] = imag

    for d, (raw, note) in enumerate(((here, note_here), (before, note_before))):
        prepare(raw, note)
        for u in range(SUB):
            white = whitened(raw, slice(u * SB, (u + 1) * SB))
            for target in range(N_FREQ):
                half = lax.rem(odd[0] + target, 2)
                row = half * (ROWS * N_FREQ // 2) + (target // 2) * ROWS + (d * SUB + u) * SHARE
                row = pl.multiple_of(row, SHARE)
                for i in range(PARTS):
                    left[pl.ds(row, SHARE), i * BAND : (i + 1) * BAND] = white[i][
                        target * SHARE : (target + 1) * SHARE
                    ]

    half_rows = ROWS * N_FREQ // 2
    for out, start in ((theirs, half_rows), (mine, 0)):
        product = lax.dot_general(
            left[start : start + half_rows, :].astype(jnp.bfloat16),
            right[...],
            (((1,), (1,)), ((), ())),
            preferred_element_type=jnp.float32,
        )
        out[...] = product.astype(jnp.bfloat16)


def dispatch_kernel(
    spot, owner, listed, parts, note_here, note_before, note_after, outgoing, right, total
):
    freq = spot[0]
    lane = lax.broadcasted_iota(jnp.int32, (1, 128), 1)
    is_valid = ((lane == VALID_LANE) | (lane == VALID_LANE + 1)).astype(jnp.float32)
    outgoing[...] = jnp.zeros_like(outgoing)
    for u in range(SUB):
        chunk = note_after[u * SB : (u + 1) * SB, :]
        for lag in range(LAGS):
            right[(u * LAGS + lag) * SB : (u * LAGS + lag + 1) * SB, :] = chunk
    for d, note in enumerate((note_here, note_before)):
        wide = note[...].astype(jnp.float32) * is_valid
        picked = []
        for u in range(SUB):
            share = wide[u * SB : u * SB + SHARE]
            for target in range(1, N_FREQ):
                rows = slice(u * SB + target * SHARE, u * SB + (target + 1) * SHARE)
                share = jnp.where(freq == target, wide[rows], share)
            picked.append(share)
        joint = lax.dot_general(
            jnp.concatenate(picked).astype(jnp.bfloat16),
            right[...],
            (((1,), (1,)), ((), ())),
            preferred_element_type=jnp.float32,
        )
        scaling = 1.0 / jnp.sqrt(jnp.maximum(joint, 1.0) * FREQS)
        half = slice(d * SUB * SHARE, (d + 1) * SUB * SHARE)
        cross = parts[0, half, :].astype(jnp.float32)
        for i in range(1, N_FREQ // 2):
            cross += parts[i, half, :].astype(jnp.float32)
        total[half, :] = cross * scaling
    for d in range(REACH):
        for u in range(SUB):
            for v in range(SUB):
                slot = (d * SUB + u) * SUB + v

                @pl.when(listed[slot] > 0)
                def _():
                    outgoing[owner[slot], d] = total[
                        (d * SUB + u) * SHARE : (d * SUB + u + 1) * SHARE,
                        v * LAGS * SB : (v + 1) * LAGS * SB,
                    ].astype(jnp.bfloat16)


def merge_kernel(received, out):
    for b in range(BLOCKS):
        out[b] = received[b, 0] + received[(b + 1) % BLOCKS, 1]


def ring(x, axis, step):
    count = lax.axis_size(axis)
    return lax.ppermute(x, axis, [(i, (i + step) % count) for i in range(count)])


def line(x, axis, step):
    count = lax.axis_size(axis)
    return lax.ppermute(
        x, axis, [(i, i + step) for i in range(count) if 0 <= i + step < count]
    )


def bf16(*shape):
    return jax.ShapeDtypeStruct(shape, jnp.bfloat16)


def params(mib):
    return pltpu.CompilerParams(vmem_limit_bytes=mib * MIB)


def body(spectra, validity, pair_mask, owners):
    chan, freq = lax.axis_index("chan"), lax.axis_index("freq")
    raw = spectra.reshape(CH, PARTS * BAND)
    raw_before = ring(raw, "chan", 1)
    raw_after = ring(raw, "chan", -1)

    low_edge, high_edge = pl.pallas_call(
        edges_kernel,
        out_shape=(bf16(CH, HALF), bf16(CH, HALF)),
        in_specs=[VMEM, VMEM],
        out_specs=(VMEM, VMEM),
        compiler_params=params(16),
        name="edges",
    )(raw, validity)
    low = line(high_edge, "freq", 1)
    high = line(low_edge, "freq", -1)
    note = jnp.concatenate(
        [low, high, validity.astype(jnp.bfloat16), jnp.zeros((CH, 62), jnp.bfloat16)], axis=1
    )
    note_before = ring(note, "chan", 1)
    note_after = ring(note, "chan", -1)

    table = lax.dynamic_index_in_dim(jnp.asarray(bin_tables()), freq, 0, keepdims=False)
    inner, spread = (jnp.asarray(a) for a in window_tables())
    half = (N_FREQ // 2, ROWS, COLS)
    mine, theirs = pl.pallas_call(
        tiles_kernel,
        out_shape=(bf16(half[0] * ROWS, COLS), bf16(half[0] * ROWS, COLS)),
        in_specs=[SMEM] + [VMEM] * 9,
        out_specs=(VMEM, VMEM),
        scratch_shapes=[
            pltpu.VMEM((CH, BAND), jnp.bfloat16),
            pltpu.VMEM((CH, 3 * BAND), jnp.float32),
            pltpu.VMEM((ROWS * N_FREQ, PARTS * BAND), jnp.float32),
            pltpu.VMEM((COLS, PARTS * BAND), jnp.bfloat16),
        ],
        compiler_params=params(40),
        name="tiles",
    )((freq % 2)[None], raw, raw_before, raw_after, note, note_before, note_after, table, inner, spread)

    count = lax.axis_size("freq")
    other = lax.ppermute(theirs, "freq", [(k, k ^ 1) for k in range(count)])
    pair = (mine.astype(jnp.float32) + other.astype(jnp.float32)).astype(jnp.bfloat16)
    groups = [[k for k in range(count) if k % 2 == core] for core in range(2)]
    parts = lax.all_to_all(
        pair.reshape(half), "freq", 0, 0, tiled=True, axis_index_groups=groups
    )

    behind = (chan + BLOCKS - 1) % BLOCKS
    listed = jnp.concatenate(
        [pair_mask[chan, 0].reshape(-1), pair_mask[behind, 1].reshape(-1)]
    )
    owner = jnp.concatenate([owners[chan, : SUB * SUB], owners[behind, SUB * SUB :]])
    outgoing = pl.pallas_call(
        dispatch_kernel,
        out_shape=bf16(BLOCKS, REACH, SHARE, LAGS * SB),
        in_specs=[SMEM] * 3 + [VMEM] * 4,
        out_specs=VMEM,
        scratch_shapes=[
            pltpu.VMEM((COLS, 128), jnp.bfloat16),
            pltpu.VMEM((ROWS, COLS), jnp.float32),
        ],
        compiler_params=params(16),
        name="dispatch",
    )(freq[None], owner, listed, parts, note, note_before, note_after)
    received = lax.all_to_all(outgoing, "chan", 0, 0, tiled=True)
    merged = pl.pallas_call(
        merge_kernel,
        out_shape=bf16(BLOCKS, SHARE, LAGS * SB),
        in_specs=[VMEM],
        out_specs=VMEM,
        compiler_params=params(8),
        name="merge",
    )(received)
    return merged[None, :, None]


def solution(mesh):
    return jax.shard_map(
        body,
        mesh=mesh,
        in_specs=(P("chan", None, None, "freq"), P("chan", None), P(), P()),
        out_specs=P("chan", None, None, "freq", None),
        check_vma=False,
    )
```

```python
import jax
import jax.numpy as jnp
import numpy as np
from jax import lax
from jax.experimental import pallas as pl
from jax.experimental.pallas import tpu as pltpu
from jax.sharding import PartitionSpec as P

FREQS = 2048
LAGS = 4
LAG_STEP = 25
HALF = 32
EPS = 1e-06

SUB = 5
SB = 64
CH = 320
BAND = 256
PARTS = 4
REACH = 2
N_FREQ = 8
BLOCKS = 64
SHARE = SB // N_FREQ
ROWS = SUB * SHARE
CHIPS = N_FREQ // 2
HALF_ROWS = CHIPS * ROWS
COLS = SUB * LAGS * SB
MIB = 1 << 20

VMEM = pl.BlockSpec(memory_space=pltpu.VMEM)
SMEM = pl.BlockSpec(memory_space=pltpu.SMEM)


def bin_tables():
    bins = np.arange(FREQS)
    lags = (np.arange(LAGS) - LAGS // 2) * LAG_STEP
    angle = np.pi * ((lags[:, None] * bins[None, :]) % (2 * FREQS)) / FREQS
    count = np.minimum(bins + HALF, FREQS - 1) - np.maximum(bins - HALF, 0) + 1
    rows = np.concatenate([np.cos(angle), np.sin(angle), np.tile(count, (8, 1))])
    return np.ascontiguousarray(
        rows.reshape(16, N_FREQ, BAND).transpose(1, 0, 2).astype(np.float32)
    )


def window_tables():
    out_bin = np.arange(BAND)[None, :]
    ranges = (np.arange(BAND), np.arange(-HALF, 0), np.arange(BAND, BAND + HALF))
    return [(np.abs(r[:, None] - out_bin) <= HALF).astype(jnp.bfloat16) for r in ranges]


def part(ref, rows, index):
    return ref[rows, index * BAND : (index + 1) * BAND].astype(jnp.float32)


def amplitude(ref, rows, weight_one, weight_two):
    first = jnp.sqrt(part(ref, rows, 0) ** 2 + part(ref, rows, 2) ** 2)
    second = jnp.sqrt(part(ref, rows, 1) ** 2 + part(ref, rows, 3) ** 2)
    return first * weight_one + second * weight_two


def edges_kernel(raw, valid, low, high):
    for start in range(0, CH, SB):
        rows = slice(start, start + SB)
        weight = valid[rows, :].astype(jnp.float32)
        level = amplitude(raw, rows, weight[:, 0:1], weight[:, 1:2]).astype(jnp.bfloat16)
        low[rows, :] = level[:, :HALF]
        high[rows, :] = level[:, BAND - HALF :]


def whiten_kernel(raw, low, high, valid, table, inner, below, above, out, level, window):
    for start in range(0, CH, SB):
        rows = slice(start, start + SB)
        weight = valid[rows, :].astype(jnp.float32)
        level[rows, :] = amplitude(raw, rows, weight[:, 0:1], weight[:, 1:2]).astype(jnp.bfloat16)
    window[...] = (
        jnp.dot(level[...], inner[...], preferred_element_type=jnp.float32)
        + jnp.dot(low[...], below[...], preferred_element_type=jnp.float32)
        + jnp.dot(high[...], above[...], preferred_element_type=jnp.float32)
    )
    for start in range(0, CH, SB):
        rows = slice(start, start + SB)
        weight = valid[rows, :].astype(jnp.float32)
        one, two = weight[:, 0:1], weight[:, 1:2]
        mean = window[rows, :] / (table[8:9, :] * jnp.maximum(one + two, 1.0))
        scale = 1.0 / (mean + EPS)
        one, two = one * scale, two * scale
        for i in range(PARTS):
            white = part(raw, rows, i) * (two if i % 2 else one)
            out[rows, i * BAND : (i + 1) * BAND] = white.astype(jnp.bfloat16)


def rotate(white, table, out):
    for u in range(SUB):
        rows = slice(u * SB, (u + 1) * SB)
        for lag in range(LAGS):
            dest = slice((u * LAGS + lag) * SB, (u * LAGS + lag + 1) * SB)
            if lag == LAGS // 2:
                out[dest, :] = white[rows, :]
                continue
            cosine, sine = table[lag : lag + 1, :], table[4 + lag : 5 + lag, :]
            for s in range(2):
                real, imag = part(white, rows, s), part(white, rows, 2 + s)
                out[dest, s * BAND : (s + 1) * BAND] = (
                    real * cosine + imag * sine
                ).astype(jnp.bfloat16)
                out[dest, (2 + s) * BAND : (3 + s) * BAND] = (
                    imag * cosine - real * sine
                ).astype(jnp.bfloat16)


def rotate_kernel(white, table, out):
    rotate(white, table, out)


def place(out, odd, block):
    for u in range(SUB):
        wide = block[u * SB : (u + 1) * SB, :].astype(jnp.float32)
        for target in range(N_FREQ):
            half = lax.rem(odd + target, 2)
            row = half * HALF_ROWS + (target // 2) * ROWS + u * SHARE
            out[pl.ds(pl.multiple_of(row, SHARE), SHARE), :] = wide[
                target * SHARE : (target + 1) * SHARE
            ]


def product(left, right):
    return lax.dot_general(
        left, right, (((1,), (1,)), ((), ())), preferred_element_type=jnp.float32
    )


def tiles_kernel(odd, before, after, right_here, table, mine, theirs, left, right_after):
    place(left, odd[0], before)
    rotate(after, table, right_after)
    rows = left[...].astype(jnp.bfloat16)
    for d, right in enumerate((right_here, right_after)):
        tile = product(rows, right[...]).astype(jnp.bfloat16)
        mine[:, d * COLS : (d + 1) * COLS] = tile[:HALF_ROWS]
        theirs[:, d * COLS : (d + 1) * COLS] = tile[HALF_ROWS:]


def gains_kernel(odd, valid_before, valid_here, valid_after, out, left, right):
    place(left, odd[0], valid_before)
    for d, valid in enumerate((valid_here, valid_after)):
        for u in range(SUB):
            chunk = valid[u * SB : (u + 1) * SB, :].astype(jnp.float32)
            for lag in range(LAGS):
                right[(u * LAGS + lag) * SB : (u * LAGS + lag + 1) * SB, :] = chunk
        joint = product(left[:HALF_ROWS, :], right[...])
        out[:, d * COLS : (d + 1) * COLS] = 1.0 / jnp.sqrt(jnp.maximum(joint, 1.0) * FREQS)


def dispatch_kernel(place_of, listed, mine, other, gain, out, total):
    out[...] = jnp.zeros_like(out)
    total[...] = (mine[...].astype(jnp.float32) + other[...].astype(jnp.float32)) * gain[...]
    for slot in range(REACH * SUB * SUB):
        d, u, v = slot // (SUB * SUB), slot // SUB % SUB, slot % SUB

        @pl.when(listed[slot] > 0)
        def _():
            for chip in range(CHIPS):
                out[place_of[slot], chip] = total[
                    chip * ROWS + u * SHARE : chip * ROWS + (u + 1) * SHARE,
                    d * COLS + v * LAGS * SB : d * COLS + (v + 1) * LAGS * SB,
                ].astype(jnp.bfloat16)


def collect_kernel(received, out):
    def block(b, _):
        total = received[b, 0].astype(jnp.float32)
        for chip in range(1, CHIPS):
            total += received[b, chip].astype(jnp.float32)
        out[b] = total.astype(jnp.bfloat16)

    lax.fori_loop(0, BLOCKS, block, None, unroll=8)


def ring(x, axis, step):
    count = lax.axis_size(axis)
    return lax.ppermute(x, axis, [(i, (i + step) % count) for i in range(count)])


def line(x, axis, step):
    count = lax.axis_size(axis)
    return lax.ppermute(
        x, axis, [(i, i + step) for i in range(count) if 0 <= i + step < count]
    )


def bf16(*shape):
    return jax.ShapeDtypeStruct(shape, jnp.bfloat16)


def kernel(fn, out_shape, inputs, scratch=(), scalars=0, mib=8):
    return pl.pallas_call(
        fn,
        out_shape=out_shape,
        in_specs=[SMEM] * scalars + [VMEM] * (inputs - scalars),
        out_specs=jax.tree.map(lambda _: VMEM, out_shape),
        scratch_shapes=[pltpu.VMEM(shape, dtype) for shape, dtype in scratch],
        compiler_params=pltpu.CompilerParams(vmem_limit_bytes=mib * MIB),
        name=fn.__name__,
    )


def body(spectra, validity, pair_mask, owners):
    f32 = jnp.float32
    chan, freq = lax.axis_index("chan"), lax.axis_index("freq")
    odd = (freq % 2)[None]
    table = lax.dynamic_index_in_dim(jnp.asarray(bin_tables()), freq, 0, keepdims=False)
    inner, below, above = (jnp.asarray(a) for a in window_tables())

    raw = spectra.reshape(CH, PARTS * BAND)
    low_edge, high_edge = kernel(edges_kernel, (bf16(CH, HALF), bf16(CH, HALF)), 2)(raw, validity)
    low = line(high_edge, "freq", 1)
    high = line(low_edge, "freq", -1)
    white = kernel(
        whiten_kernel,
        bf16(CH, PARTS * BAND),
        8,
        [((CH, BAND), jnp.bfloat16), ((CH, BAND), f32)],
    )(raw, low, high, validity, table, inner, below, above)
    before = ring(white, "chan", 1)
    after = ring(white, "chan", -1)

    right_here = kernel(rotate_kernel, bf16(COLS, PARTS * BAND), 2)(white, table)
    valid, _ = lax.optimization_barrier((validity, right_here))
    valid_before = ring(valid, "chan", 1)
    valid_after = ring(valid, "chan", -1)
    before, after, valid_before, valid_after = lax.optimization_barrier(
        (before, after, valid_before, valid_after)
    )
    gain = kernel(
        gains_kernel,
        jax.ShapeDtypeStruct((HALF_ROWS, REACH * COLS), f32),
        4,
        [((2 * HALF_ROWS, 2), f32), ((COLS, 2), f32)],
        scalars=1,
    )(odd, valid_before, valid, valid_after)

    half = bf16(HALF_ROWS, REACH * COLS)
    mine, theirs = kernel(
        tiles_kernel,
        (half, half),
        5,
        [((2 * HALF_ROWS, PARTS * BAND), f32), ((COLS, PARTS * BAND), jnp.bfloat16)],
        scalars=1,
        mib=20,
    )(odd, before, after, right_here, table)
    other = lax.ppermute(theirs, "freq", [(k, k ^ 1) for k in range(N_FREQ)])

    block = (chan + BLOCKS - 1) % BLOCKS
    listed = pair_mask[block].reshape(-1)
    place_of = (owners[block] + BLOCKS - 1) % BLOCKS
    outgoing = kernel(
        dispatch_kernel,
        bf16(BLOCKS, CHIPS, SHARE, LAGS * SB),
        5,
        [((HALF_ROWS, REACH * COLS), f32)],
        scalars=2,
    )(place_of, listed, mine, other, gain)
    groups = [
        [
            (b + 1) % BLOCKS * N_FREQ + 2 * chip + core
            for b in range(BLOCKS)
            for chip in range(CHIPS)
        ]
        for core in range(2)
    ]
    received = lax.all_to_all(
        outgoing.reshape(BLOCKS * CHIPS, SHARE, LAGS * SB),
        ("chan", "freq"),
        0,
        0,
        tiled=True,
        axis_index_groups=groups,
    )
    merged = kernel(collect_kernel, bf16(BLOCKS, SHARE, LAGS * SB), 1)(
        received.reshape(BLOCKS, CHIPS, SHARE, LAGS * SB)
    )
    return merged[None, :, None]


def solution(mesh):
    return jax.shard_map(
        body,
        mesh=mesh,
        in_specs=(P("chan", None, None, "freq"), P("chan", None), P(), P()),
        out_specs=P("chan", None, None, "freq", None),
        check_vma=False,
    )
```

```python
import jax
import jax.numpy as jnp
import numpy as np
from jax import lax
from jax.experimental import pallas as pl
from jax.experimental.pallas import tpu as pltpu
from jax.sharding import PartitionSpec as P

FREQS = 2048
LAGS = 4
LAG_STEP = 25
HALF = 32
EPS = 1e-06

SUB = 5
SB = 64
CH = 320
BAND = 256
PARTS = 4
REACH = 2
N_FREQ = 8
BLOCKS = 64
SHARE = SB // N_FREQ
ROWS = SUB * SHARE
CHIPS = N_FREQ // 2
HALF_ROWS = CHIPS * ROWS
WIDE = 384
COLS = SUB * LAGS * SB
MIB = 1 << 20

VMEM = pl.BlockSpec(memory_space=pltpu.VMEM)
SMEM = pl.BlockSpec(memory_space=pltpu.SMEM)


def bin_tables():
    bins = np.arange(FREQS)
    lags = (np.arange(LAGS) - LAGS // 2) * LAG_STEP
    angle = np.pi * ((lags[:, None] * bins[None, :]) % (2 * FREQS)) / FREQS
    count = np.minimum(bins + HALF, FREQS - 1) - np.maximum(bins - HALF, 0) + 1
    rows = np.concatenate([np.cos(angle), np.sin(angle), np.tile(count, (8, 1))])
    return np.ascontiguousarray(
        rows.reshape(16, N_FREQ, BAND).transpose(1, 0, 2).astype(np.float32)
    )


def part(ref, rows, index):
    return ref[rows, index * BAND : (index + 1) * BAND].astype(jnp.float32)


def amplitudes(block, rows):
    return [
        jnp.sqrt(part(block, rows, i) ** 2 + part(block, rows, i + 2) ** 2) for i in range(2)
    ]


def edges_kernel(odd, raw, inside, across):
    for start in range(0, CH, SB):
        rows = slice(start, start + SB)
        both = amplitudes(raw, rows)
        low = jnp.concatenate([x[:, :HALF] for x in both], axis=1)
        high = jnp.concatenate([x[:, BAND - HALF :] for x in both], axis=1)
        inside[rows, :] = jnp.where(odd[0] > 0, low, high).astype(jnp.bfloat16)
        across[rows, :] = jnp.where(odd[0] > 0, high, low).astype(jnp.bfloat16)


def validity_kernel(valid, tail, columns, wide):
    wide[...] = jnp.zeros_like(wide)
    wide[:2, :CH] = valid[...].astype(jnp.float32)
    tail[...] = wide[...].astype(jnp.bfloat16)
    columns[...] = wide[:8, :WIDE].T


def whiten_kernel(odd, raw, inside, across, tail, columns, table, out, level, window):
    out[CH:, :] = tail[...]
    weights = columns[...]
    for start in range(0, CH, SB):
        rows = slice(start, start + SB)
        one, two = amplitudes(raw, rows)
        level[rows, :] = (one * weights[rows, 0:1] + two * weights[rows, 1:2]).astype(jnp.bfloat16)

    def total(levels, chosen):
        return jnp.dot(
            levels[...], chosen.astype(jnp.bfloat16), preferred_element_type=jnp.float32
        )

    source, out_bin = (lax.broadcasted_iota(jnp.int32, (BAND, BAND), d) for d in range(2))
    sums = total(level, jnp.where(jnp.abs(source - out_bin) <= HALF, 1.0, 0.0))
    lane, edge_out = (lax.broadcasted_iota(jnp.int32, (2 * HALF, BAND), d) for d in range(2))
    for s in range(2):
        edge = lane - s * HALF
        ours = (edge >= 0) & (edge < HALF)
        below = jnp.where(ours & (edge_out <= edge), 1.0, 0.0)
        above = jnp.where(ours & (edge_out >= edge + BAND - HALF), 1.0, 0.0)
        beside = total(inside, jnp.where(odd[0] > 0, below, above))
        beside += total(across, jnp.where(odd[0] > 0, above, below))
        sums += beside * weights[:CH, s : s + 1]
    window[...] = sums
    for start in range(0, CH, SB):
        rows = slice(start, start + SB)
        one, two = weights[rows, 0:1], weights[rows, 1:2]
        mean = window[rows, :] / (table[8:9, :] * jnp.maximum(one + two, 1.0))
        scale = 1.0 / (mean + EPS)
        one, two = one * scale, two * scale
        for i in range(PARTS):
            white = part(raw, rows, i) * (two if i % 2 else one)
            out[rows, i * BAND : (i + 1) * BAND] = white.astype(jnp.bfloat16)


def rotate(white, table, out):
    for u in range(SUB):
        rows = slice(u * SB, (u + 1) * SB)
        for lag in range(LAGS):
            dest = slice((u * LAGS + lag) * SB, (u * LAGS + lag + 1) * SB)
            if lag == LAGS // 2:
                out[dest, :] = white[rows, :]
                continue
            cosine, sine = table[lag : lag + 1, :], table[4 + lag : 5 + lag, :]
            for s in range(2):
                real, imag = part(white, rows, s), part(white, rows, 2 + s)
                out[dest, s * BAND : (s + 1) * BAND] = (
                    real * cosine + imag * sine
                ).astype(jnp.bfloat16)
                out[dest, (2 + s) * BAND : (3 + s) * BAND] = (
                    imag * cosine - real * sine
                ).astype(jnp.bfloat16)


def rotate_kernel(white, table, out):
    rotate(white, table, out)


def place(out, odd, block):
    for u in range(SUB):
        wide = block[u * SB : (u + 1) * SB, :].astype(jnp.float32)
        for target in range(N_FREQ):
            half = lax.rem(odd + target, 2)
            row = half * HALF_ROWS + (target // 2) * ROWS + u * SHARE
            out[pl.ds(pl.multiple_of(row, SHARE), SHARE), :] = wide[
                target * SHARE : (target + 1) * SHARE
            ]


def product(left, right):
    return lax.dot_general(
        left, right, (((1,), (1,)), ((), ())), preferred_element_type=jnp.float32
    )


def near_kernel(odd, place_of, listed, before, right, rows, mine, theirs, left):
    place(left, odd[0], before)
    rows[...] = left[...].astype(jnp.bfloat16)
    tile = product(rows[...], right[...]).astype(jnp.bfloat16)
    mine[...] = tile[:HALF_ROWS]
    theirs[...] = tile[HALF_ROWS:]


def far_kernel(rows, after, near, table, theirs, right):
    rotate(after, table, right)
    theirs[:, :COLS] = near[...]
    theirs[:, COLS:] = product(rows[HALF_ROWS:, :], right[...]).astype(jnp.bfloat16)


def rest_kernel(rows, right, mine):
    mine[...] = product(rows[:HALF_ROWS, :], right[...]).astype(jnp.bfloat16)


def gains_kernel(odd, before, here, after, out, left, right):
    def valid(block):
        return block[CH : CH + 16, : PARTS * 128].astype(jnp.float32)[:8]

    place(left, odd[0], valid(before).T)
    for d, block in enumerate((here, after)):
        flags = valid(block)
        for v in range(SUB):
            chunk = flags[:, v * SB : (v + 1) * SB]
            right[:, d * COLS + v * LAGS * SB : d * COLS + (v + 1) * LAGS * SB] = (
                jnp.concatenate([chunk] * LAGS, axis=1)
            )
    joint = jnp.dot(left[:HALF_ROWS, :], right[...], preferred_element_type=jnp.float32)
    out[...] = jnp.where(joint > 1.5, (2 * FREQS) ** -0.5, FREQS**-0.5)


def dispatch_kernel(place_of, listed, mine, mine_far, other, gain, out, total):
    out[...] = jnp.zeros_like(out)
    for d, ours in enumerate((mine, mine_far)):
        lanes = slice(d * COLS, (d + 1) * COLS)
        pair = ours[...].astype(jnp.float32) + other[:, lanes].astype(jnp.float32)
        total[:, lanes] = pair * gain[:, lanes]
    for slot in range(REACH * SUB * SUB):
        d, u, v = slot // (SUB * SUB), slot // SUB % SUB, slot % SUB

        @pl.when(listed[slot] > 0)
        def _():
            for chip in range(CHIPS):
                out[place_of[slot], chip] = total[
                    chip * ROWS + u * SHARE : chip * ROWS + (u + 1) * SHARE,
                    d * COLS + v * LAGS * SB : d * COLS + (v + 1) * LAGS * SB,
                ].astype(jnp.bfloat16)


def collect_kernel(received, out):
    def block(b, _):
        source = lax.rem(b + 1, BLOCKS)
        total = received[source, 0].astype(jnp.float32)
        for chip in range(1, CHIPS):
            total += received[source, chip].astype(jnp.float32)
        out[b] = total.astype(jnp.bfloat16)

    lax.fori_loop(0, BLOCKS, block, None, unroll=8)


def ring(x, axis, step):
    count = lax.axis_size(axis)
    return lax.ppermute(x, axis, [(i, (i + step) % count) for i in range(count)])


def swap(x, first):
    pairs = [(k, k + 1) for k in range(first, N_FREQ - 1, 2)]
    return lax.ppermute(x, "freq", pairs + [(k, i) for i, k in pairs])


def bf16(*shape):
    return jax.ShapeDtypeStruct(shape, jnp.bfloat16)


def kernel(fn, out_shape, inputs, scratch=(), scalars=0, mib=8):
    return pl.pallas_call(
        fn,
        out_shape=out_shape,
        in_specs=[SMEM] * scalars + [VMEM] * (inputs - scalars),
        out_specs=jax.tree.map(lambda _: VMEM, out_shape),
        scratch_shapes=[pltpu.VMEM(shape, dtype) for shape, dtype in scratch],
        compiler_params=pltpu.CompilerParams(vmem_limit_bytes=mib * MIB),
        name=fn.__name__,
    )


def body(spectra, validity, pair_mask, owners):
    f32 = jnp.float32
    chan, freq = lax.axis_index("chan"), lax.axis_index("freq")
    odd = (freq % 2)[None]
    table = lax.dynamic_index_in_dim(jnp.asarray(bin_tables()), freq, 0, keepdims=False)
    raw = spectra.reshape(CH, PARTS * BAND)
    edge = bf16(CH, 2 * HALF)
    to_inside, to_across = kernel(edges_kernel, (edge, edge), 2, scalars=1)(odd, raw)
    across = swap(to_across, 1)
    inside = swap(to_inside, 0)
    tail, columns = kernel(
        validity_kernel,
        (bf16(16, PARTS * BAND), jax.ShapeDtypeStruct((WIDE, 8), f32)),
        1,
        [((16, PARTS * BAND), f32)],
    )(validity.T)
    white = kernel(
        whiten_kernel,
        bf16(CH + 16, PARTS * BAND),
        7,
        [((CH, BAND), jnp.bfloat16), ((CH, BAND), f32)],
        scalars=1,
    )(odd, raw, inside, across, tail, columns, table)
    before = ring(white, "chan", 1)
    after = ring(white, "chan", -1)

    right_here = kernel(rotate_kernel, bf16(COLS, PARTS * BAND), 2)(white, table)
    gain = kernel(
        gains_kernel,
        jax.ShapeDtypeStruct((HALF_ROWS, REACH * COLS), f32),
        4,
        [((2 * HALF_ROWS, 8), f32), ((8, REACH * COLS), f32)],
        scalars=1,
    )(odd, before, white, after)

    block = (chan + BLOCKS - 1) % BLOCKS
    listed = pair_mask[block].reshape(-1)
    place_of = owners[block]
    half = bf16(HALF_ROWS, COLS)
    right = bf16(COLS, PARTS * BAND)
    rows, mine, near = kernel(
        near_kernel,
        (bf16(2 * HALF_ROWS, PARTS * BAND), half, half),
        5,
        [((2 * HALF_ROWS, PARTS * BAND), f32)],
        scalars=3,
        mib=10,
    )(odd, place_of, listed, before, right_here)
    theirs, right_after = kernel(far_kernel, (bf16(HALF_ROWS, REACH * COLS), right), 4)(
        rows, after, near, table
    )
    mine_far = kernel(rest_kernel, half, 2)(rows, right_after)
    other = lax.ppermute(theirs, "freq", [(k, k ^ 1) for k in range(N_FREQ)])

    outgoing = kernel(
        dispatch_kernel,
        bf16(BLOCKS, CHIPS, SHARE, LAGS * SB),
        6,
        [((HALF_ROWS, REACH * COLS), f32)],
        scalars=2,
    )(place_of, listed, mine, mine_far, other, gain)
    groups = [
        [
            b * N_FREQ + 2 * chip + core
            for b in range(BLOCKS)
            for chip in range(CHIPS)
        ]
        for core in range(2)
    ]
    received = lax.all_to_all(
        outgoing.reshape(BLOCKS * CHIPS, SHARE, LAGS * SB),
        ("chan", "freq"),
        0,
        0,
        tiled=True,
        axis_index_groups=groups,
    )
    merged = kernel(collect_kernel, bf16(BLOCKS, SHARE, LAGS * SB), 1)(
        received.reshape(BLOCKS, CHIPS, SHARE, LAGS * SB)
    )
    return merged[None, :, None]


def solution(mesh):
    return jax.shard_map(
        body,
        mesh=mesh,
        in_specs=(P("chan", None, None, "freq"), P("chan", None), P(), P()),
        out_specs=P("chan", None, None, "freq", None),
        check_vma=False,
    )
```

```python
import jax
import jax.numpy as jnp
import numpy as np
from jax import lax
from jax.experimental import pallas as pl
from jax.experimental.pallas import tpu as pltpu
from jax.sharding import PartitionSpec as P

FREQS = 2048
LAGS = 4
LAG_STEP = 25
HALF = 32
EPS = 1e-06

SUB = 5
SB = 64
CH = 320
BAND = 256
PARTS = 4
REACH = 2
N_FREQ = 8
BLOCKS = 64
SHARE = SB // N_FREQ
ROWS = SUB * SHARE
CHIPS = N_FREQ // 2
HALF_ROWS = CHIPS * ROWS
WIDE = 384
COLS = SUB * LAGS * SB
MIB = 1 << 20

VMEM = pl.BlockSpec(memory_space=pltpu.VMEM)
SMEM = pl.BlockSpec(memory_space=pltpu.SMEM)


def lag_tables():
    lags = (np.arange(LAGS) - LAGS // 2) * LAG_STEP
    angle = np.pi * ((lags[:, None] * np.arange(FREQS)[None, :]) % (2 * FREQS)) / FREQS
    rows = np.concatenate([np.cos(angle), np.sin(angle)])
    return np.ascontiguousarray(
        rows.reshape(8, N_FREQ, BAND).transpose(1, 0, 2).astype(np.float32)
    )


def part(ref, rows, index):
    return ref[rows, index * BAND : (index + 1) * BAND].astype(jnp.float32)


def amplitudes(block, rows):
    return [
        jnp.sqrt(part(block, rows, i) ** 2 + part(block, rows, i + 2) ** 2) for i in range(2)
    ]


def edge(raw, rows, high):
    both = amplitudes(raw, rows)
    ends = [
        jnp.concatenate([x[:, start : start + HALF] for x in both], axis=1)
        for start in (0, BAND - HALF)
    ]
    return jnp.where(high > 0, ends[1], ends[0]).astype(jnp.bfloat16)


def across_kernel(odd, raw, out):
    for start in range(0, CH, SB):
        rows = slice(start, start + SB)
        out[rows, :] = edge(raw, rows, odd[0])


def inside_kernel(odd, raw, across, valid, out, tail, columns, wide):
    for start in range(0, CH, SB):
        rows = slice(start, start + SB)
        out[rows, :] = edge(raw, rows, 1 - odd[0])
    wide[...] = jnp.zeros_like(wide)
    wide[:2, :CH] = valid[...].astype(jnp.float32)
    tail[...] = wide[...].astype(jnp.bfloat16)
    columns[...] = wide[:8, :WIDE].T


def whiten_kernel(spot, raw, inside, across, tail, columns, table, out, level, window):
    out[CH:, :] = tail[...]
    weights = columns[...]
    odd = lax.rem(spot[0], 2)
    bins = spot[0] * BAND + lax.broadcasted_iota(jnp.int32, (1, BAND), 1)
    count = jnp.minimum(bins + HALF, FREQS - 1) - jnp.maximum(bins - HALF, 0) + 1
    count = count.astype(jnp.float32)
    for start in range(0, CH, SB):
        rows = slice(start, start + SB)
        one, two = amplitudes(raw, rows)
        level[rows, :] = (one * weights[rows, 0:1] + two * weights[rows, 1:2]).astype(jnp.bfloat16)

    def total(levels, chosen):
        return jnp.dot(
            levels[...], chosen.astype(jnp.bfloat16), preferred_element_type=jnp.float32
        )

    source, out_bin = (lax.broadcasted_iota(jnp.int32, (BAND, BAND), d) for d in range(2))
    sums = total(level, jnp.where(jnp.abs(source - out_bin) <= HALF, 1.0, 0.0))
    lane, edge_out = (lax.broadcasted_iota(jnp.int32, (2 * HALF, BAND), d) for d in range(2))
    for s in range(2):
        edge = lane - s * HALF
        ours = (edge >= 0) & (edge < HALF)
        below = jnp.where(ours & (edge_out <= edge), 1.0, 0.0)
        above = jnp.where(ours & (edge_out >= edge + BAND - HALF), 1.0, 0.0)
        beside = total(inside, jnp.where(odd > 0, below, above))
        beside += total(across, jnp.where(odd > 0, above, below))
        sums += beside * weights[:CH, s : s + 1]
    window[...] = sums
    for start in range(0, CH, SB):
        rows = slice(start, start + SB)
        one, two = weights[rows, 0:1], weights[rows, 1:2]
        mean = window[rows, :] / (count * jnp.maximum(one + two, 1.0))
        scale = 1.0 / (mean + EPS)
        one, two = one * scale, two * scale
        for i in range(PARTS):
            white = part(raw, rows, i) * (two if i % 2 else one)
            out[rows, i * BAND : (i + 1) * BAND] = white.astype(jnp.bfloat16)


def rotate(white, table, out):
    for u in range(SUB):
        rows = slice(u * SB, (u + 1) * SB)
        for lag in range(LAGS):
            dest = slice((u * LAGS + lag) * SB, (u * LAGS + lag + 1) * SB)
            if lag == LAGS // 2:
                out[dest, :] = white[rows, :]
                continue
            cosine, sine = table[lag : lag + 1, :], table[4 + lag : 5 + lag, :]
            for s in range(2):
                real, imag = part(white, rows, s), part(white, rows, 2 + s)
                out[dest, s * BAND : (s + 1) * BAND] = (
                    real * cosine + imag * sine
                ).astype(jnp.bfloat16)
                out[dest, (2 + s) * BAND : (3 + s) * BAND] = (
                    imag * cosine - real * sine
                ).astype(jnp.bfloat16)


def rotate_kernel(white, table, out):
    rotate(white, table, out)


def place(out, odd, block):
    for u in range(SUB):
        wide = block[u * SB : (u + 1) * SB, :].astype(jnp.float32)
        for target in range(N_FREQ):
            half = lax.rem(odd + target, 2)
            row = half * HALF_ROWS + (target // 2) * ROWS + u * SHARE
            out[pl.ds(pl.multiple_of(row, SHARE), SHARE), :] = wide[
                target * SHARE : (target + 1) * SHARE
            ]


def product(left, right):
    return lax.dot_general(
        left, right, (((1,), (1,)), ((), ())), preferred_element_type=jnp.float32
    )


def near_kernel(odd, place_of, listed, before, right, rows, mine, theirs, left):
    place(left, odd[0], before)
    rows[...] = left[...].astype(jnp.bfloat16)
    tile = product(rows[...], right[...]).astype(jnp.bfloat16)
    mine[...] = tile[:HALF_ROWS]
    theirs[...] = tile[HALF_ROWS:]


def far_kernel(rows, after, near, table, theirs, right):
    rotate(after, table, right)
    theirs[:, :COLS] = near[...]
    theirs[:, COLS:] = product(rows[HALF_ROWS:, :], right[...]).astype(jnp.bfloat16)


def rest_kernel(rows, right, mine):
    mine[...] = product(rows[:HALF_ROWS, :], right[...]).astype(jnp.bfloat16)


def gains_kernel(odd, before, here, after, out, left, right):
    def valid(block):
        return block[CH : CH + 16, : PARTS * 128].astype(jnp.float32)[:8]

    place(left, odd[0], valid(before).T)
    for d, block in enumerate((here, after)):
        flags = valid(block)
        for v in range(SUB):
            chunk = flags[:, v * SB : (v + 1) * SB]
            right[:, d * COLS + v * LAGS * SB : d * COLS + (v + 1) * LAGS * SB] = (
                jnp.concatenate([chunk] * LAGS, axis=1)
            )
    joint = jnp.dot(left[:HALF_ROWS, :], right[...], preferred_element_type=jnp.float32)
    out[...] = jnp.where(joint > 1.5, (2 * FREQS) ** -0.5, FREQS**-0.5)


def dispatch_kernel(place_of, listed, mine, mine_far, other, gain, out, total):
    out[...] = jnp.zeros_like(out)
    for d, ours in enumerate((mine, mine_far)):
        lanes = slice(d * COLS, (d + 1) * COLS)
        pair = ours[...].astype(jnp.float32) + other[:, lanes].astype(jnp.float32)
        total[:, lanes] = pair * gain[:, lanes]
    for slot in range(REACH * SUB * SUB):
        d, u, v = slot // (SUB * SUB), slot // SUB % SUB, slot % SUB

        @pl.when(listed[slot] > 0)
        def _():
            for chip in range(CHIPS):
                out[place_of[slot], chip] = total[
                    chip * ROWS + u * SHARE : chip * ROWS + (u + 1) * SHARE,
                    d * COLS + v * LAGS * SB : d * COLS + (v + 1) * LAGS * SB,
                ].astype(jnp.bfloat16)


def collect_kernel(received, out):
    def block(b, _):
        source = lax.rem(b + 1, BLOCKS)
        total = received[source, 0].astype(jnp.float32)
        for chip in range(1, CHIPS):
            total += received[source, chip].astype(jnp.float32)
        out[b] = total.astype(jnp.bfloat16)

    lax.fori_loop(0, BLOCKS, block, None, unroll=8)


def ring(x, axis, step):
    count = lax.axis_size(axis)
    return lax.ppermute(x, axis, [(i, (i + step) % count) for i in range(count)])


def swap(x, first):
    pairs = [(k, k + 1) for k in range(first, N_FREQ - 1, 2)]
    return lax.ppermute(x, "freq", pairs + [(k, i) for i, k in pairs])


def bf16(*shape):
    return jax.ShapeDtypeStruct(shape, jnp.bfloat16)


def kernel(fn, out_shape, inputs, scratch=(), scalars=0, mib=8):
    return pl.pallas_call(
        fn,
        out_shape=out_shape,
        in_specs=[SMEM] * scalars + [VMEM] * (inputs - scalars),
        out_specs=jax.tree.map(lambda _: VMEM, out_shape),
        scratch_shapes=[pltpu.VMEM(shape, dtype) for shape, dtype in scratch],
        compiler_params=pltpu.CompilerParams(vmem_limit_bytes=mib * MIB),
        name=fn.__name__,
    )


def body(spectra, validity, pair_mask, owners):
    f32 = jnp.float32
    chan, freq = lax.axis_index("chan"), lax.axis_index("freq")
    odd = (freq % 2)[None]
    table = lax.dynamic_index_in_dim(jnp.asarray(lag_tables()), freq, 0, keepdims=False)
    raw = spectra.reshape(CH, PARTS * BAND)
    edges = bf16(CH, 2 * HALF)
    to_across = kernel(across_kernel, edges, 2, scalars=1)(odd, raw)
    across = swap(to_across, 1)
    to_inside, tail, columns = kernel(
        inside_kernel,
        (edges, bf16(16, PARTS * BAND), jax.ShapeDtypeStruct((WIDE, 8), f32)),
        4,
        [((16, PARTS * BAND), f32)],
        scalars=1,
    )(odd, raw, to_across, validity.T)
    inside = swap(to_inside, 0)
    block = bf16(CH + 16, PARTS * BAND)
    white = kernel(
        whiten_kernel, block, 7, [((CH, BAND), jnp.bfloat16), ((CH, BAND), f32)], scalars=1
    )(freq[None], raw, inside, across, tail, columns, table)
    after = ring(white, "chan", -1)
    before = ring(white, "chan", 1)
    right_here = kernel(rotate_kernel, bf16(COLS, PARTS * BAND), 2)(white, table)

    gain = kernel(
        gains_kernel,
        jax.ShapeDtypeStruct((HALF_ROWS, REACH * COLS), f32),
        4,
        [((2 * HALF_ROWS, 8), f32), ((8, REACH * COLS), f32)],
        scalars=1,
    )(odd, before, white, after)

    source = (chan + BLOCKS - 1) % BLOCKS
    listed = pair_mask[source].reshape(-1)
    place_of = owners[source]
    half = bf16(HALF_ROWS, COLS)
    right = bf16(COLS, PARTS * BAND)
    rows, mine, near = kernel(
        near_kernel,
        (bf16(2 * HALF_ROWS, PARTS * BAND), half, half),
        5,
        [((2 * HALF_ROWS, PARTS * BAND), f32)],
        scalars=3,
        mib=10,
    )(odd, place_of, listed, before, right_here)
    theirs, right_after = kernel(far_kernel, (bf16(HALF_ROWS, REACH * COLS), right), 4)(
        rows, after, near, table
    )
    mine_far = kernel(rest_kernel, half, 2)(rows, right_after)
    other = lax.ppermute(theirs, "freq", [(k, k ^ 1) for k in range(N_FREQ)])

    outgoing = kernel(
        dispatch_kernel,
        bf16(BLOCKS, CHIPS, SHARE, LAGS * SB),
        6,
        [((HALF_ROWS, REACH * COLS), f32)],
        scalars=2,
    )(place_of, listed, mine, mine_far, other, gain)
    groups = [
        [
            b * N_FREQ + 2 * chip + core
            for b in range(BLOCKS)
            for chip in range(CHIPS)
        ]
        for core in range(2)
    ]
    received = lax.all_to_all(
        outgoing.reshape(BLOCKS * CHIPS, SHARE, LAGS * SB),
        ("chan", "freq"),
        0,
        0,
        tiled=True,
        axis_index_groups=groups,
    )
    merged = kernel(collect_kernel, bf16(BLOCKS, SHARE, LAGS * SB), 1)(
        received.reshape(BLOCKS, CHIPS, SHARE, LAGS * SB)
    )
    return merged[None, :, None]


def solution(mesh):
    return jax.shard_map(
        body,
        mesh=mesh,
        in_specs=(P("chan", None, None, "freq"), P("chan", None), P(), P()),
        out_specs=P("chan", None, None, "freq", None),
        check_vma=False,
    )
```

```python
import jax
import jax.numpy as jnp
import numpy as np
from jax import lax
from jax.experimental import pallas as pl
from jax.experimental.pallas import tpu as pltpu
from jax.sharding import PartitionSpec as P

FREQS = 2048
LAGS = 4
LAG_STEP = 25
HALF = 32
EPS = 1e-06

SUB = 5
SB = 64
CH = 320
BAND = 256
PARTS = 4
REACH = 2
N_FREQ = 8
BLOCKS = 64
SHARE = SB // N_FREQ
ROWS = SUB * SHARE
CHIPS = N_FREQ // 2
HALF_ROWS = CHIPS * ROWS
WIDE = 384
COLS = SUB * LAGS * SB
MIB = 1 << 20

VMEM = pl.BlockSpec(memory_space=pltpu.VMEM)
SMEM = pl.BlockSpec(memory_space=pltpu.SMEM)


def lag_tables():
    lags = (np.arange(LAGS) - LAGS // 2) * LAG_STEP
    angle = np.pi * ((lags[:, None] * np.arange(FREQS)[None, :]) % (2 * FREQS)) / FREQS
    rows = np.concatenate([np.cos(angle), np.sin(angle)])
    return np.ascontiguousarray(
        rows.reshape(8, N_FREQ, BAND).transpose(1, 0, 2).astype(np.float32)
    )


def part(ref, rows, index):
    return ref[rows, index * BAND : (index + 1) * BAND].astype(jnp.float32)


def amplitudes(block, rows):
    return [
        jnp.sqrt(part(block, rows, i) ** 2 + part(block, rows, i + 2) ** 2) for i in range(2)
    ]


def edge(raw, rows, high):
    both = amplitudes(raw, rows)
    ends = [
        jnp.concatenate([x[:, start : start + HALF] for x in both], axis=1)
        for start in (0, BAND - HALF)
    ]
    return jnp.where(high > 0, ends[1], ends[0]).astype(jnp.bfloat16)


def across_kernel(odd, raw, out):
    for start in range(0, CH, SB):
        rows = slice(start, start + SB)
        out[rows, :] = edge(raw, rows, odd[0])


def inside_kernel(odd, raw, across, out):
    for start in range(0, CH, SB):
        rows = slice(start, start + SB)
        out[rows, :] = edge(raw, rows, 1 - odd[0])


def validity_kernel(inside, valid, tail, columns, wide):
    wide[...] = jnp.zeros_like(wide)
    wide[:2, :CH] = valid[...].astype(jnp.float32)
    tail[...] = wide[...].astype(jnp.bfloat16)
    columns[...] = wide[:8, :WIDE].T


def whiten_kernel(spot, raw, across, inside, tail, columns, table, out, level, window):
    out[CH:, :] = tail[...]
    weights = columns[...]
    odd = lax.rem(spot[0], 2)
    bins = spot[0] * BAND + lax.broadcasted_iota(jnp.int32, (1, BAND), 1)
    count = jnp.minimum(bins + HALF, FREQS - 1) - jnp.maximum(bins - HALF, 0) + 1
    count = count.astype(jnp.float32)
    for start in range(0, CH, SB):
        rows = slice(start, start + SB)
        one, two = amplitudes(raw, rows)
        level[rows, :] = (one * weights[rows, 0:1] + two * weights[rows, 1:2]).astype(jnp.bfloat16)

    def total(levels, chosen):
        return jnp.dot(
            levels[...], chosen.astype(jnp.bfloat16), preferred_element_type=jnp.float32
        )

    source, out_bin = (lax.broadcasted_iota(jnp.int32, (BAND, BAND), d) for d in range(2))
    sums = total(level, jnp.where(jnp.abs(source - out_bin) <= HALF, 1.0, 0.0))
    lane, edge_out = (lax.broadcasted_iota(jnp.int32, (2 * HALF, BAND), d) for d in range(2))
    for s in range(2):
        edge = lane - s * HALF
        ours = (edge >= 0) & (edge < HALF)
        below = jnp.where(ours & (edge_out <= edge), 1.0, 0.0)
        above = jnp.where(ours & (edge_out >= edge + BAND - HALF), 1.0, 0.0)
        beside = total(inside, jnp.where(odd > 0, below, above))
        beside += total(across, jnp.where(odd > 0, above, below))
        sums += beside * weights[:CH, s : s + 1]
    window[...] = sums
    for start in range(0, CH, SB):
        rows = slice(start, start + SB)
        one, two = weights[rows, 0:1], weights[rows, 1:2]
        mean = window[rows, :] / (count * jnp.maximum(one + two, 1.0))
        scale = 1.0 / (mean + EPS)
        one, two = one * scale, two * scale
        for i in range(PARTS):
            white = part(raw, rows, i) * (two if i % 2 else one)
            out[rows, i * BAND : (i + 1) * BAND] = white.astype(jnp.bfloat16)


def rotate(white, table, out):
    for u in range(SUB):
        rows = slice(u * SB, (u + 1) * SB)
        for lag in range(LAGS):
            dest = slice((u * LAGS + lag) * SB, (u * LAGS + lag + 1) * SB)
            if lag == LAGS // 2:
                out[dest, :] = white[rows, :]
                continue
            cosine, sine = table[lag : lag + 1, :], table[4 + lag : 5 + lag, :]
            for s in range(2):
                real, imag = part(white, rows, s), part(white, rows, 2 + s)
                out[dest, s * BAND : (s + 1) * BAND] = (
                    real * cosine + imag * sine
                ).astype(jnp.bfloat16)
                out[dest, (2 + s) * BAND : (3 + s) * BAND] = (
                    imag * cosine - real * sine
                ).astype(jnp.bfloat16)


def rotate_kernel(white, table, out):
    rotate(white, table, out)


def place(out, odd, block):
    for u in range(SUB):
        wide = block[u * SB : (u + 1) * SB, :].astype(jnp.float32)
        for target in range(N_FREQ):
            half = lax.rem(odd + target, 2)
            row = half * HALF_ROWS + (target // 2) * ROWS + u * SHARE
            out[pl.ds(pl.multiple_of(row, SHARE), SHARE), :] = wide[
                target * SHARE : (target + 1) * SHARE
            ]


def product(left, right):
    return lax.dot_general(
        left, right, (((1,), (1,)), ((), ())), preferred_element_type=jnp.float32
    )


def near_kernel(odd, place_of, listed, before, right, rows, mine, theirs, left):
    place(left, odd[0], before)
    rows[...] = left[...].astype(jnp.bfloat16)
    tile = product(rows[...], right[...]).astype(jnp.bfloat16)
    mine[...] = tile[:HALF_ROWS]
    theirs[...] = tile[HALF_ROWS:]


def far_kernel(rows, after, table, near_other, near_gain, mine, theirs, right):
    rotate(after, table, right)
    tile = product(rows[...], right[...]).astype(jnp.bfloat16)
    mine[...] = tile[:HALF_ROWS]
    theirs[...] = tile[HALF_ROWS:]


def gains_kernel(odd, before, block, near, out, left, right):
    def flags(x):
        return x[CH : CH + 16, :WIDE].astype(jnp.float32)[:8]

    place(left, odd[0], flags(before).T)
    valid = flags(block)
    for v in range(SUB):
        chunk = valid[:, v * SB : (v + 1) * SB]
        right[:, v * LAGS * SB : (v + 1) * LAGS * SB] = jnp.concatenate([chunk] * LAGS, axis=1)
    joint = jnp.dot(left[:HALF_ROWS, :], right[...], preferred_element_type=jnp.float32)
    out[...] = jnp.where(joint > 1.5, (2 * FREQS) ** -0.5, FREQS**-0.5)


def dispatch(place_of, listed, d, ours, other, gain, out, total):
    total[...] = (ours[...].astype(jnp.float32) + other[...].astype(jnp.float32)) * gain[...]
    for u in range(SUB):
        for v in range(SUB):
            slot = (d * SUB + u) * SUB + v

            @pl.when(listed[slot] > 0)
            def _():
                for chip in range(CHIPS):
                    out[place_of[slot], chip] = total[
                        chip * ROWS + u * SHARE : chip * ROWS + (u + 1) * SHARE,
                        v * LAGS * SB : (v + 1) * LAGS * SB,
                    ].astype(jnp.bfloat16)


def near_dispatch_kernel(place_of, listed, ours, other, gain, theirs, out, total):
    out[...] = jnp.zeros_like(out)
    dispatch(place_of, listed, 0, ours, other, gain, out, total)


def far_dispatch_kernel(place_of, listed, ours, other, gain, near, out, total):
    dispatch(place_of, listed, 1, ours, other, gain, out, total)


def collect_kernel(received, out):
    def block(b, _):
        source = lax.rem(b + 1, BLOCKS)
        total = received[source, 0].astype(jnp.float32)
        for chip in range(1, CHIPS):
            total += received[source, chip].astype(jnp.float32)
        out[b] = total.astype(jnp.bfloat16)

    lax.fori_loop(0, BLOCKS, block, None, unroll=8)


def ring(x, axis, step):
    count = lax.axis_size(axis)
    return lax.ppermute(x, axis, [(i, (i + step) % count) for i in range(count)])


def swap(x, first):
    pairs = [(k, k + 1) for k in range(first, N_FREQ - 1, 2)]
    return lax.ppermute(x, "freq", pairs + [(k, i) for i, k in pairs])


def bf16(*shape):
    return jax.ShapeDtypeStruct(shape, jnp.bfloat16)


def kernel(fn, out_shape, inputs, scratch=(), scalars=0, mib=8, aliases=()):
    return pl.pallas_call(
        fn,
        out_shape=out_shape,
        in_specs=[SMEM] * scalars + [VMEM] * (inputs - scalars),
        out_specs=jax.tree.map(lambda _: VMEM, out_shape),
        scratch_shapes=[pltpu.VMEM(shape, dtype) for shape, dtype in scratch],
        compiler_params=pltpu.CompilerParams(vmem_limit_bytes=mib * MIB),
        input_output_aliases=dict(aliases),
        name=fn.__name__,
    )


def body(spectra, validity, pair_mask, owners):
    f32 = jnp.float32
    chan, freq = lax.axis_index("chan"), lax.axis_index("freq")
    odd = (freq % 2)[None]
    table = lax.dynamic_index_in_dim(jnp.asarray(lag_tables()), freq, 0, keepdims=False)
    raw = spectra.reshape(CH, PARTS * BAND)
    edges = bf16(CH, 2 * HALF)
    to_across = kernel(across_kernel, edges, 2, scalars=1)(odd, raw)
    across = swap(to_across, 1)
    to_inside = kernel(inside_kernel, edges, 3, scalars=1)(odd, raw, to_across)
    tail, columns = kernel(
        validity_kernel,
        (bf16(16, PARTS * BAND), jax.ShapeDtypeStruct((WIDE, 8), f32)),
        2,
        [((16, PARTS * BAND), f32)],
    )(to_inside, validity.T)
    inside = swap(to_inside, 0)
    block = bf16(CH + 16, PARTS * BAND)
    white = kernel(
        whiten_kernel, block, 7, [((CH, BAND), jnp.bfloat16), ((CH, BAND), f32)], scalars=1
    )(freq[None], raw, across, inside, tail, columns, table)
    after = ring(white, "chan", -1)
    before = ring(white, "chan", 1)
    right_here = kernel(rotate_kernel, bf16(COLS, PARTS * BAND), 2)(white, table)

    source = (chan + BLOCKS - 1) % BLOCKS
    listed = pair_mask[source].reshape(-1)
    place_of = owners[source]
    half = bf16(HALF_ROWS, COLS)
    rows, mine, near = kernel(
        near_kernel,
        (bf16(2 * HALF_ROWS, PARTS * BAND), half, half),
        5,
        [((2 * HALF_ROWS, PARTS * BAND), f32)],
        scalars=3,
        mib=10,
    )(odd, place_of, listed, before, right_here)
    def gain(block, mark):
        return kernel(
            gains_kernel,
            jax.ShapeDtypeStruct((HALF_ROWS, COLS), f32),
            4,
            [((2 * HALF_ROWS, 8), f32), ((8, COLS), f32)],
            scalars=1,
        )(odd, before, block, mark)

    pairs = [(k, k ^ 1) for k in range(N_FREQ)]
    near_other = lax.ppermute(near, "freq", pairs)
    near_gain = gain(white, near)
    mine_far, theirs = kernel(
        far_kernel, (half, half), 5, [((COLS, PARTS * BAND), jnp.bfloat16)]
    )(rows, after, table, near_other, near_gain)
    far_other = lax.ppermute(theirs, "freq", pairs)
    far_gain = gain(after, theirs)
    sending = bf16(BLOCKS, CHIPS, SHARE, LAGS * SB)
    total = [((HALF_ROWS, COLS), f32)]
    near_sent = kernel(near_dispatch_kernel, sending, 6, total, scalars=2)(
        place_of, listed, mine, near_other, near_gain, theirs
    )
    outgoing = kernel(far_dispatch_kernel, sending, 6, total, scalars=2, aliases={5: 0})(
        place_of, listed, mine_far, far_other, far_gain, near_sent
    )
    groups = [
        [
            b * N_FREQ + 2 * chip + core
            for b in range(BLOCKS)
            for chip in range(CHIPS)
        ]
        for core in range(2)
    ]
    received = lax.all_to_all(
        outgoing.reshape(BLOCKS * CHIPS, SHARE, LAGS * SB),
        ("chan", "freq"),
        0,
        0,
        tiled=True,
        axis_index_groups=groups,
    )
    merged = kernel(collect_kernel, bf16(BLOCKS, SHARE, LAGS * SB), 1)(
        received.reshape(BLOCKS, CHIPS, SHARE, LAGS * SB)
    )
    return merged[None, :, None]


def solution(mesh):
    return jax.shard_map(
        body,
        mesh=mesh,
        in_specs=(P("chan", None, None, "freq"), P("chan", None), P(), P()),
        out_specs=P("chan", None, None, "freq", None),
        check_vma=False,
    )
```

```python
import jax
import jax.numpy as jnp
import numpy as np
from jax import lax
from jax.experimental import pallas as pl
from jax.experimental.pallas import tpu as pltpu
from jax.sharding import PartitionSpec as P

FREQS = 2048
LAGS = 4
LAG_STEP = 25
HALF = 32
EPS = 1e-06

SUB = 5
SB = 64
CH = 320
BAND = 256
PARTS = 4
REACH = 2
N_FREQ = 8
BLOCKS = 64
SHARE = SB // N_FREQ
ROWS = SUB * SHARE
CHIPS = N_FREQ // 2
HALF_ROWS = CHIPS * ROWS
WIDE = 384
COLS = SUB * LAGS * SB
MIB = 1 << 20

VMEM = pl.BlockSpec(memory_space=pltpu.VMEM)
SMEM = pl.BlockSpec(memory_space=pltpu.SMEM)


def lag_tables():
    lags = (np.arange(LAGS) - LAGS // 2) * LAG_STEP
    angle = np.pi * ((lags[:, None] * np.arange(FREQS)[None, :]) % (2 * FREQS)) / FREQS
    rows = np.concatenate([np.cos(angle), np.sin(angle)])
    return np.ascontiguousarray(
        rows.reshape(8, N_FREQ, BAND).transpose(1, 0, 2).astype(np.float32)
    )


def part(ref, rows, index):
    return ref[rows, index * BAND : (index + 1) * BAND].astype(jnp.float32)


def amplitudes(block, rows):
    return [
        jnp.sqrt(part(block, rows, i) ** 2 + part(block, rows, i + 2) ** 2) for i in range(2)
    ]


def edge(raw, rows, high):
    both = amplitudes(raw, rows)
    ends = [
        jnp.concatenate([x[:, start : start + HALF] for x in both], axis=1)
        for start in (0, BAND - HALF)
    ]
    return jnp.where(high > 0, ends[1], ends[0]).astype(jnp.bfloat16)


def across_kernel(odd, raw, out):
    for start in range(0, CH, SB):
        rows = slice(start, start + SB)
        out[rows, :] = edge(raw, rows, odd[0])


def inside_kernel(odd, raw, across, out):
    for start in range(0, CH, SB):
        rows = slice(start, start + SB)
        out[rows, :] = edge(raw, rows, 1 - odd[0])


def validity_kernel(inside, valid, tail, columns, wide):
    wide[...] = jnp.zeros_like(wide)
    wide[:2, :CH] = valid[...].astype(jnp.float32)
    tail[...] = wide[...].astype(jnp.bfloat16)
    columns[...] = wide[:8, :WIDE].T


def whiten_kernel(spot, raw, across, inside, tail, columns, table, out, level, window):
    out[CH:, :] = tail[...]
    weights = columns[...]
    odd = lax.rem(spot[0], 2)
    bins = spot[0] * BAND + lax.broadcasted_iota(jnp.int32, (1, BAND), 1)
    count = jnp.minimum(bins + HALF, FREQS - 1) - jnp.maximum(bins - HALF, 0) + 1
    count = count.astype(jnp.float32)
    for start in range(0, CH, SB):
        rows = slice(start, start + SB)
        one, two = amplitudes(raw, rows)
        level[rows, :] = (one * weights[rows, 0:1] + two * weights[rows, 1:2]).astype(jnp.bfloat16)

    def total(levels, chosen):
        return jnp.dot(
            levels[...], chosen.astype(jnp.bfloat16), preferred_element_type=jnp.float32
        )

    source, out_bin = (lax.broadcasted_iota(jnp.int32, (BAND, BAND), d) for d in range(2))
    sums = total(level, jnp.where(jnp.abs(source - out_bin) <= HALF, 1.0, 0.0))
    lane, edge_out = (lax.broadcasted_iota(jnp.int32, (2 * HALF, BAND), d) for d in range(2))
    for s in range(2):
        edge = lane - s * HALF
        ours = (edge >= 0) & (edge < HALF)
        below = jnp.where(ours & (edge_out <= edge), 1.0, 0.0)
        above = jnp.where(ours & (edge_out >= edge + BAND - HALF), 1.0, 0.0)
        beside = total(inside, jnp.where(odd > 0, below, above))
        beside += total(across, jnp.where(odd > 0, above, below))
        sums += beside * weights[:CH, s : s + 1]
    window[...] = sums
    for start in range(0, CH, SB):
        rows = slice(start, start + SB)
        one, two = weights[rows, 0:1], weights[rows, 1:2]
        mean = window[rows, :] / (count * jnp.maximum(one + two, 1.0))
        scale = 1.0 / (mean + EPS)
        one, two = one * scale, two * scale
        for i in range(PARTS):
            white = part(raw, rows, i) * (two if i % 2 else one)
            out[rows, i * BAND : (i + 1) * BAND] = white.astype(jnp.bfloat16)


def plain(block):
    return lambda rows, lanes=slice(None): block[rows, lanes].astype(jnp.float32)


def chosen(odd, even_block, odd_block):
    def read(rows, lanes=slice(None)):
        both = [x[rows, lanes].astype(jnp.float32) for x in (even_block, odd_block)]
        return jnp.where(odd > 0, both[1], both[0])

    return read


def rotate(read, table, out):
    for u in range(SUB):
        for s in range(2):
            lanes = [slice(i * BAND, (i + 1) * BAND) for i in (s, 2 + s)]
            real, imag = (read(slice(u * SB, (u + 1) * SB), x) for x in lanes)
            for lag in range(LAGS):
                dest = slice((u * LAGS + lag) * SB, (u * LAGS + lag + 1) * SB)
                turned = real, imag
                if lag != LAGS // 2:
                    cosine, sine = table[lag : lag + 1, :], table[4 + lag : 5 + lag, :]
                    turned = real * cosine + imag * sine, imag * cosine - real * sine
                for x, value in zip(lanes, turned):
                    out[dest, x] = value.astype(jnp.bfloat16)


def rotate_kernel(white, table, out):
    rotate(plain(white), table, out)


def place(out, odd, read):
    for u in range(SUB):
        wide = read(slice(u * SB, (u + 1) * SB))
        for target in range(N_FREQ):
            half = lax.rem(odd + target, 2)
            row = half * HALF_ROWS + (target // 2) * ROWS + u * SHARE
            out[pl.ds(pl.multiple_of(row, SHARE), SHARE), :] = wide[
                target * SHARE : (target + 1) * SHARE
            ]


def product(left, right):
    return lax.dot_general(
        left, right, (((1,), (1,)), ((), ())), preferred_element_type=jnp.float32
    )


def prepare(odd, behind, block, table, left, right_after):
    @pl.when(behind)
    def _():
        place(left, odd, plain(block))

    @pl.when(jnp.logical_not(behind))
    def _():
        rotate(plain(block), table, right_after)


def first_kernel(odd, place_of, listed, first, right_here, table, left, right_after):
    prepare(odd[0], odd[0] == 0, first, table, left, right_after)


def second_kernel(
    odd, left_in, right_in, second, right_here, table, left, right_after, mine, theirs
):
    prepare(odd[0], odd[0] != 0, second, table, left, right_after)
    rows = left[...].astype(jnp.bfloat16)
    for d, right in enumerate((right_here, right_after)):
        tile = product(rows, right[...]).astype(jnp.bfloat16)
        mine[:, d * COLS : (d + 1) * COLS] = tile[:HALF_ROWS]
        theirs[:, d * COLS : (d + 1) * COLS] = tile[HALF_ROWS:]


def gains_kernel(odd, first, here, second, theirs, out, left, right):
    def flags(read):
        return read(slice(CH, CH + 16), slice(0, WIDE))[:8]

    columns = flags(chosen(odd[0], first, second)).T
    place(left, odd[0], lambda rows: columns[rows])
    for d, read in enumerate((plain(here), chosen(odd[0], second, first))):
        valid = flags(read)
        for v in range(SUB):
            chunk = valid[:, v * SB : (v + 1) * SB]
            right[:, d * COLS + v * LAGS * SB : d * COLS + (v + 1) * LAGS * SB] = (
                jnp.concatenate([chunk] * LAGS, axis=1)
            )
    joint = jnp.dot(left[:HALF_ROWS, :], right[...], preferred_element_type=jnp.float32)
    out[...] = jnp.where(joint > 1.5, (2 * FREQS) ** -0.5, FREQS**-0.5)


def dispatch_kernel(place_of, listed, mine, other, gain, out, total):
    out[...] = jnp.zeros_like(out)
    total[...] = (mine[...].astype(jnp.float32) + other[...].astype(jnp.float32)) * gain[...]
    for slot in range(REACH * SUB * SUB):
        d, u, v = slot // (SUB * SUB), slot // SUB % SUB, slot % SUB

        @pl.when(listed[slot] > 0)
        def _():
            for chip in range(CHIPS):
                out[place_of[slot], chip] = total[
                    chip * ROWS + u * SHARE : chip * ROWS + (u + 1) * SHARE,
                    d * COLS + v * LAGS * SB : d * COLS + (v + 1) * LAGS * SB,
                ].astype(jnp.bfloat16)


def collect_kernel(received, out):
    def block(b, _):
        source = lax.rem(b + 1, BLOCKS)
        total = received[source, 0].astype(jnp.float32)
        for chip in range(1, CHIPS):
            total += received[source, chip].astype(jnp.float32)
        out[b] = total.astype(jnp.bfloat16)

    lax.fori_loop(0, BLOCKS, block, None, unroll=8)


def spread(x, forward):
    route = [
        (b * N_FREQ + k, (b + (1 if k % 2 == forward else -1)) % BLOCKS * N_FREQ + k)
        for b in range(BLOCKS)
        for k in range(N_FREQ)
    ]
    return lax.ppermute(x, ("chan", "freq"), route)


def swap(x, first):
    pairs = [(k, k + 1) for k in range(first, N_FREQ - 1, 2)]
    return lax.ppermute(x, "freq", pairs + [(k, i) for i, k in pairs])


def bf16(*shape):
    return jax.ShapeDtypeStruct(shape, jnp.bfloat16)


def kernel(fn, out_shape, inputs, scratch=(), scalars=0, mib=8, aliases=()):
    return pl.pallas_call(
        fn,
        out_shape=out_shape,
        in_specs=[SMEM] * scalars + [VMEM] * (inputs - scalars),
        out_specs=jax.tree.map(lambda _: VMEM, out_shape),
        scratch_shapes=[pltpu.VMEM(shape, dtype) for shape, dtype in scratch],
        compiler_params=pltpu.CompilerParams(vmem_limit_bytes=mib * MIB),
        input_output_aliases=dict(aliases),
        name=fn.__name__,
    )


def body(spectra, validity, pair_mask, owners):
    f32 = jnp.float32
    chan, freq = lax.axis_index("chan"), lax.axis_index("freq")
    odd = (freq % 2)[None]
    table = lax.dynamic_index_in_dim(jnp.asarray(lag_tables()), freq, 0, keepdims=False)
    raw = spectra.reshape(CH, PARTS * BAND)
    edges = bf16(CH, 2 * HALF)
    to_across = kernel(across_kernel, edges, 2, scalars=1)(odd, raw)
    across = swap(to_across, 1)
    to_inside = kernel(inside_kernel, edges, 3, scalars=1)(odd, raw, to_across)
    tail, columns = kernel(
        validity_kernel,
        (bf16(16, PARTS * BAND), jax.ShapeDtypeStruct((WIDE, 8), f32)),
        2,
        [((16, PARTS * BAND), f32)],
    )(to_inside, validity.T)
    inside = swap(to_inside, 0)
    block = bf16(CH + 16, PARTS * BAND)
    white = kernel(
        whiten_kernel, block, 7, [((CH, BAND), jnp.bfloat16), ((CH, BAND), f32)], scalars=1
    )(freq[None], raw, across, inside, tail, columns, table)
    first = spread(white, 0)
    second = spread(white, 1)
    right_here = kernel(rotate_kernel, bf16(COLS, PARTS * BAND), 2)(white, table)

    source = (chan + BLOCKS - 1) % BLOCKS
    listed = pair_mask[source].reshape(-1)
    place_of = owners[source]
    half = bf16(HALF_ROWS, REACH * COLS)
    kept = (
        jax.ShapeDtypeStruct((2 * HALF_ROWS, PARTS * BAND), f32),
        bf16(COLS, PARTS * BAND),
    )
    left, right_after = kernel(first_kernel, kept, 6, scalars=3)(
        odd, place_of, listed, first, right_here, table
    )
    _, _, mine, theirs = kernel(
        second_kernel, (*kept, half, half), 6, scalars=1, aliases={1: 0, 2: 1}
    )(odd, left, right_after, second, right_here, table)
    other = lax.ppermute(theirs, "freq", [(k, k ^ 1) for k in range(N_FREQ)])
    gain = kernel(
        gains_kernel,
        jax.ShapeDtypeStruct((HALF_ROWS, REACH * COLS), f32),
        5,
        [((2 * HALF_ROWS, 8), f32), ((8, REACH * COLS), f32)],
        scalars=1,
    )(odd, first, white, second, theirs)
    outgoing = kernel(
        dispatch_kernel,
        bf16(BLOCKS, CHIPS, SHARE, LAGS * SB),
        5,
        [((HALF_ROWS, REACH * COLS), f32)],
        scalars=2,
    )(place_of, listed, mine, other, gain)
    groups = [
        [
            b * N_FREQ + 2 * chip + core
            for b in range(BLOCKS)
            for chip in range(CHIPS)
        ]
        for core in range(2)
    ]
    received = lax.all_to_all(
        outgoing.reshape(BLOCKS * CHIPS, SHARE, LAGS * SB),
        ("chan", "freq"),
        0,
        0,
        tiled=True,
        axis_index_groups=groups,
    )
    merged = kernel(collect_kernel, bf16(BLOCKS, SHARE, LAGS * SB), 1)(
        received.reshape(BLOCKS, CHIPS, SHARE, LAGS * SB)
    )
    return merged[None, :, None]


def solution(mesh):
    return jax.shard_map(
        body,
        mesh=mesh,
        in_specs=(P("chan", None, None, "freq"), P("chan", None), P(), P()),
        out_specs=P("chan", None, None, "freq", None),
        check_vma=False,
    )
```

```python
import jax
import jax.numpy as jnp
import numpy as np
from jax import lax
from jax.experimental import pallas as pl
from jax.experimental.pallas import tpu as pltpu
from jax.sharding import PartitionSpec as P

FREQS = 2048
LAGS = 4
LAG_STEP = 25
HALF = 32
EPS = 1e-06

SUB = 5
SB = 64
CH = 320
BAND = 256
PARTS = 4
REACH = 2
N_FREQ = 8
BLOCKS = 64
SHARE = SB // N_FREQ
ROWS = SUB * SHARE
CHIPS = N_FREQ // 2
HALF_ROWS = CHIPS * ROWS
WIDE = 384
COLS = SUB * LAGS * SB
MIB = 1 << 20

VMEM = pl.BlockSpec(memory_space=pltpu.VMEM)
SMEM = pl.BlockSpec(memory_space=pltpu.SMEM)


def lag_tables():
    lags = (np.arange(LAGS) - LAGS // 2) * LAG_STEP
    angle = np.pi * ((lags[:, None] * np.arange(FREQS)[None, :]) % (2 * FREQS)) / FREQS
    rows = np.concatenate([np.cos(angle), np.sin(angle)])
    return np.ascontiguousarray(
        rows.reshape(8, N_FREQ, BAND).transpose(1, 0, 2).astype(np.float32)
    )


def part(ref, rows, index):
    return ref[rows, index * BAND : (index + 1) * BAND].astype(jnp.float32)


def amplitudes(block, rows):
    return [
        jnp.sqrt(part(block, rows, i) ** 2 + part(block, rows, i + 2) ** 2) for i in range(2)
    ]


def edge(raw, rows, high):
    both = amplitudes(raw, rows)
    ends = [
        jnp.concatenate([x[:, start : start + HALF] for x in both], axis=1)
        for start in (0, BAND - HALF)
    ]
    return jnp.where(high > 0, ends[1], ends[0]).astype(jnp.bfloat16)


def across_kernel(odd, raw, out):
    for start in range(0, CH, SB):
        rows = slice(start, start + SB)
        out[rows, :] = edge(raw, rows, odd[0])


def inside_kernel(odd, raw, across, out):
    for start in range(0, CH, SB):
        rows = slice(start, start + SB)
        out[rows, :] = edge(raw, rows, 1 - odd[0])


def validity_kernel(inside, valid, tail, columns, wide):
    wide[...] = jnp.zeros_like(wide)
    wide[:2, :CH] = valid[...].astype(jnp.float32)
    tail[...] = wide[...].astype(jnp.bfloat16)
    columns[...] = wide[:8, :WIDE].T


def whiten_kernel(spot, raw, across, inside, tail, columns, table, out, level, window):
    out[CH:, :] = tail[...]
    weights = columns[...]
    odd = lax.rem(spot[0], 2)
    bins = spot[0] * BAND + lax.broadcasted_iota(jnp.int32, (1, BAND), 1)
    count = jnp.minimum(bins + HALF, FREQS - 1) - jnp.maximum(bins - HALF, 0) + 1
    count = count.astype(jnp.float32)
    for start in range(0, CH, SB):
        rows = slice(start, start + SB)
        one, two = amplitudes(raw, rows)
        level[rows, :] = (one * weights[rows, 0:1] + two * weights[rows, 1:2]).astype(jnp.bfloat16)

    def total(levels, chosen):
        return jnp.dot(
            levels[...], chosen.astype(jnp.bfloat16), preferred_element_type=jnp.float32
        )

    source, out_bin = (lax.broadcasted_iota(jnp.int32, (BAND, BAND), d) for d in range(2))
    sums = total(level, jnp.where(jnp.abs(source - out_bin) <= HALF, 1.0, 0.0))
    lane, edge_out = (lax.broadcasted_iota(jnp.int32, (2 * HALF, BAND), d) for d in range(2))
    for s in range(2):
        edge = lane - s * HALF
        ours = (edge >= 0) & (edge < HALF)
        below = jnp.where(ours & (edge_out <= edge), 1.0, 0.0)
        above = jnp.where(ours & (edge_out >= edge + BAND - HALF), 1.0, 0.0)
        beside = total(inside, jnp.where(odd > 0, below, above))
        beside += total(across, jnp.where(odd > 0, above, below))
        sums += beside * weights[:CH, s : s + 1]
    window[...] = sums
    for start in range(0, CH, SB):
        rows = slice(start, start + SB)
        one, two = weights[rows, 0:1], weights[rows, 1:2]
        mean = window[rows, :] / (count * jnp.maximum(one + two, 1.0))
        scale = 1.0 / (mean + EPS)
        one, two = one * scale, two * scale
        for i in range(PARTS):
            white = part(raw, rows, i) * (two if i % 2 else one)
            out[rows, i * BAND : (i + 1) * BAND] = white.astype(jnp.bfloat16)


def plain(block):
    return lambda rows, lanes=slice(None): block[rows, lanes].astype(jnp.float32)


def chosen(odd, even_block, odd_block):
    def read(rows, lanes=slice(None)):
        both = [x[rows, lanes].astype(jnp.float32) for x in (even_block, odd_block)]
        return jnp.where(odd > 0, both[1], both[0])

    return read


def rotate(read, table, out):
    for u in range(SUB):
        for s in range(2):
            lanes = [slice(i * BAND, (i + 1) * BAND) for i in (s, 2 + s)]
            real, imag = (read(slice(u * SB, (u + 1) * SB), x) for x in lanes)
            for lag in range(LAGS):
                dest = slice((u * LAGS + lag) * SB, (u * LAGS + lag + 1) * SB)
                turned = real, imag
                if lag != LAGS // 2:
                    cosine, sine = table[lag : lag + 1, :], table[4 + lag : 5 + lag, :]
                    turned = real * cosine + imag * sine, imag * cosine - real * sine
                for x, value in zip(lanes, turned):
                    out[dest, x] = value.astype(jnp.bfloat16)


def rotate_kernel(white, table, out):
    rotate(plain(white), table, out)


def place(out, odd, read):
    for u in range(SUB):
        wide = read(slice(u * SB, (u + 1) * SB))
        for target in range(N_FREQ):
            half = lax.rem(odd + target, 2)
            row = half * HALF_ROWS + (target // 2) * ROWS + u * SHARE
            out[pl.ds(pl.multiple_of(row, SHARE), SHARE), :] = wide[
                target * SHARE : (target + 1) * SHARE
            ]


def product(left, right):
    return lax.dot_general(
        left, right, (((1,), (1,)), ((), ())), preferred_element_type=jnp.float32
    )


def prepare(odd, behind, block, table, left, right_after):
    @pl.when(behind)
    def _():
        place(left, odd, plain(block))

    @pl.when(jnp.logical_not(behind))
    def _():
        rotate(plain(block), table, right_after)


def first_kernel(odd, place_of, listed, first, right_here, table, left, right_after):
    prepare(odd[0], odd[0] == 0, first, table, left, right_after)


def second_kernel(
    odd, left_in, right_in, second, right_here, table, left, right_after, mine, theirs
):
    prepare(odd[0], odd[0] != 0, second, table, left, right_after)
    rows = left[...].astype(jnp.bfloat16)
    for d, right in enumerate((right_here, right_after)):
        tile = product(rows, right[...]).astype(jnp.bfloat16)
        mine[:, d * COLS : (d + 1) * COLS] = tile[:HALF_ROWS]
        theirs[:, d * COLS : (d + 1) * COLS] = tile[HALF_ROWS:]


def gains_kernel(odd, first, here, second, theirs, out, left, right):
    def flags(read):
        return read(slice(CH, CH + 16), slice(0, WIDE))[:8]

    columns = flags(chosen(odd[0], first, second)).T
    place(left, odd[0], lambda rows: columns[rows])
    for d, read in enumerate((plain(here), chosen(odd[0], second, first))):
        valid = flags(read)
        for v in range(SUB):
            chunk = valid[:, v * SB : (v + 1) * SB]
            right[:, d * COLS + v * LAGS * SB : d * COLS + (v + 1) * LAGS * SB] = (
                jnp.concatenate([chunk] * LAGS, axis=1)
            )
    joint = jnp.dot(left[:HALF_ROWS, :], right[...], preferred_element_type=jnp.float32)
    out[...] = jnp.where(joint > 1.5, (2 * FREQS) ** -0.5, FREQS**-0.5)


def dispatch_kernel(place_of, listed, mine, other, gain, out, total):
    out[...] = jnp.zeros_like(out)
    total[...] = (mine[...].astype(jnp.float32) + other[...].astype(jnp.float32)) * gain[...]
    for slot in range(REACH * SUB * SUB):
        d, u, v = slot // (SUB * SUB), slot // SUB % SUB, slot % SUB
        keep = listed[slot].astype(jnp.float32)
        for chip in range(CHIPS):
            tile = total[
                chip * ROWS + u * SHARE : chip * ROWS + (u + 1) * SHARE,
                d * COLS + v * LAGS * SB : d * COLS + (v + 1) * LAGS * SB,
            ]
            out[place_of[slot], chip] = (tile * keep).astype(jnp.bfloat16)


def collect_kernel(received, out, sums, done):
    half = BLOCKS // 2
    copies = []
    for part_of in range(2):
        for b in range(part_of * half, (part_of + 1) * half):
            total = received[(b + 1) % BLOCKS, 0].astype(jnp.float32)
            for chip in range(1, CHIPS):
                total += received[(b + 1) % BLOCKS, chip].astype(jnp.float32)
            sums[b] = total.astype(jnp.bfloat16)
        rows = pl.ds(part_of * half, half)
        copies.append(pltpu.make_async_copy(sums.at[rows], out.at[rows], done.at[part_of]))
        copies[-1].start()
    for copy in copies:
        copy.wait()


def spread(x, forward):
    route = [
        (b * N_FREQ + k, (b + (1 if k % 2 == forward else -1)) % BLOCKS * N_FREQ + k)
        for b in range(BLOCKS)
        for k in range(N_FREQ)
    ]
    return lax.ppermute(x, ("chan", "freq"), route)


def swap(x, first):
    pairs = [(k, k + 1) for k in range(first, N_FREQ - 1, 2)]
    return lax.ppermute(x, "freq", pairs + [(k, i) for i, k in pairs])


def bf16(*shape):
    return jax.ShapeDtypeStruct(shape, jnp.bfloat16)


def kernel(fn, out_shape, inputs, scratch=(), scalars=0, mib=8, aliases=()):
    return pl.pallas_call(
        fn,
        out_shape=out_shape,
        in_specs=[SMEM] * scalars + [VMEM] * (inputs - scalars),
        out_specs=jax.tree.map(lambda _: VMEM, out_shape),
        scratch_shapes=[pltpu.VMEM(shape, dtype) for shape, dtype in scratch],
        compiler_params=pltpu.CompilerParams(vmem_limit_bytes=mib * MIB),
        input_output_aliases=dict(aliases),
        name=fn.__name__,
    )


def body(spectra, validity, pair_mask, owners):
    f32 = jnp.float32
    chan, freq = lax.axis_index("chan"), lax.axis_index("freq")
    odd = (freq % 2)[None]
    table = lax.dynamic_index_in_dim(jnp.asarray(lag_tables()), freq, 0, keepdims=False)
    raw = spectra.reshape(CH, PARTS * BAND)
    edges = bf16(CH, 2 * HALF)
    to_across = kernel(across_kernel, edges, 2, scalars=1)(odd, raw)
    across = swap(to_across, 1)
    to_inside = kernel(inside_kernel, edges, 3, scalars=1)(odd, raw, to_across)
    tail, columns = kernel(
        validity_kernel,
        (bf16(16, PARTS * BAND), jax.ShapeDtypeStruct((WIDE, 8), f32)),
        2,
        [((16, PARTS * BAND), f32)],
    )(to_inside, validity.T)
    inside = swap(to_inside, 0)
    block = bf16(CH + 16, PARTS * BAND)
    white = kernel(
        whiten_kernel, block, 7, [((CH, BAND), jnp.bfloat16), ((CH, BAND), f32)], scalars=1
    )(freq[None], raw, across, inside, tail, columns, table)
    first = spread(white, 0)
    second = spread(white, 1)
    right_here = kernel(rotate_kernel, bf16(COLS, PARTS * BAND), 2)(white, table)

    source = (chan + BLOCKS - 1) % BLOCKS
    listed = pair_mask[source].reshape(-1)
    place_of = owners[source]
    half = bf16(HALF_ROWS, REACH * COLS)
    kept = (
        jax.ShapeDtypeStruct((2 * HALF_ROWS, PARTS * BAND), f32),
        bf16(COLS, PARTS * BAND),
    )
    left, right_after = kernel(first_kernel, kept, 6, scalars=3)(
        odd, place_of, listed, first, right_here, table
    )
    _, _, mine, theirs = kernel(
        second_kernel, (*kept, half, half), 6, scalars=1, aliases={1: 0, 2: 1}
    )(odd, left, right_after, second, right_here, table)
    other = lax.ppermute(theirs, "freq", [(k, k ^ 1) for k in range(N_FREQ)])
    gain = kernel(
        gains_kernel,
        jax.ShapeDtypeStruct((HALF_ROWS, REACH * COLS), f32),
        5,
        [((2 * HALF_ROWS, 8), f32), ((8, REACH * COLS), f32)],
        scalars=1,
    )(odd, first, white, second, theirs)
    outgoing = kernel(
        dispatch_kernel,
        bf16(BLOCKS, CHIPS, SHARE, LAGS * SB),
        5,
        [((HALF_ROWS, REACH * COLS), f32)],
        scalars=2,
    )(place_of, listed, mine, other, gain)
    groups = [
        [
            b * N_FREQ + 2 * chip + core
            for b in range(BLOCKS)
            for chip in range(CHIPS)
        ]
        for core in range(2)
    ]
    received = lax.all_to_all(
        outgoing.reshape(BLOCKS * CHIPS, SHARE, LAGS * SB),
        ("chan", "freq"),
        0,
        0,
        tiled=True,
        axis_index_groups=groups,
    )
    merged = pl.pallas_call(
        collect_kernel,
        out_shape=bf16(BLOCKS, SHARE, LAGS * SB),
        in_specs=[VMEM],
        out_specs=pl.BlockSpec(memory_space=pl.ANY),
        scratch_shapes=[
            pltpu.VMEM((BLOCKS, SHARE, LAGS * SB), jnp.bfloat16),
            pltpu.SemaphoreType.DMA((2,)),
        ],
        compiler_params=pltpu.CompilerParams(vmem_limit_bytes=4 * MIB),
        name="collect_kernel",
    )(received.reshape(BLOCKS, CHIPS, SHARE, LAGS * SB))
    return merged[None, :, None]


def solution(mesh):
    return jax.shard_map(
        body,
        mesh=mesh,
        in_specs=(P("chan", None, None, "freq"), P("chan", None), P(), P()),
        out_specs=P("chan", None, None, "freq", None),
        check_vma=False,
    )
```

```python
import jax
import jax.numpy as jnp
import numpy as np
from jax import lax
from jax.experimental import pallas as pl
from jax.experimental.pallas import tpu as pltpu
from jax.sharding import PartitionSpec as P

FREQS = 2048
LAGS = 4
LAG_STEP = 25
HALF = 32
EPS = 1e-06

SUB = 5
SB = 64
CH = 320
BAND = 256
PARTS = 4
REACH = 2
N_FREQ = 8
BLOCKS = 64
SHARE = SB // N_FREQ
ROWS = SUB * SHARE
CHIPS = N_FREQ // 2
HALF_ROWS = CHIPS * ROWS
WIDE = 384
COLS = SUB * LAGS * SB
MIB = 1 << 20

VMEM = pl.BlockSpec(memory_space=pltpu.VMEM)
SMEM = pl.BlockSpec(memory_space=pltpu.SMEM)


def lag_tables():
    lags = (np.arange(LAGS) - LAGS // 2) * LAG_STEP
    angle = np.pi * ((lags[:, None] * np.arange(FREQS)[None, :]) % (2 * FREQS)) / FREQS
    rows = np.concatenate([np.cos(angle), np.sin(angle)])
    return np.ascontiguousarray(
        rows.reshape(8, N_FREQ, BAND).transpose(1, 0, 2).astype(np.float32)
    )


def part(ref, rows, index):
    return ref[rows, index * BAND : (index + 1) * BAND].astype(jnp.float32)


def amplitudes(block, rows):
    return [
        jnp.sqrt(part(block, rows, i) ** 2 + part(block, rows, i + 2) ** 2) for i in range(2)
    ]


def edge(raw, rows, high):
    both = amplitudes(raw, rows)
    ends = [
        jnp.concatenate([x[:, start : start + HALF] for x in both], axis=1)
        for start in (0, BAND - HALF)
    ]
    return jnp.where(high > 0, ends[1], ends[0]).astype(jnp.bfloat16)


def across_kernel(odd, raw, out):
    for start in range(0, CH, SB):
        rows = slice(start, start + SB)
        out[rows, :] = edge(raw, rows, odd[0])


def inside_kernel(odd, raw, across, out):
    for start in range(0, CH, SB):
        rows = slice(start, start + SB)
        out[rows, :] = edge(raw, rows, 1 - odd[0])


def validity_kernel(inside, valid, tail, columns, wide):
    wide[...] = jnp.zeros_like(wide)
    wide[:2, :CH] = valid[...].astype(jnp.float32)
    tail[...] = wide[...].astype(jnp.bfloat16)
    columns[...] = wide[:8, :WIDE].T


def whiten_kernel(spot, raw, across, inside, tail, columns, table, out, level, window):
    out[CH:, :] = tail[...]
    weights = columns[...]
    odd = lax.rem(spot[0], 2)
    bins = spot[0] * BAND + lax.broadcasted_iota(jnp.int32, (1, BAND), 1)
    count = jnp.minimum(bins + HALF, FREQS - 1) - jnp.maximum(bins - HALF, 0) + 1
    count = count.astype(jnp.float32)
    for start in range(0, CH, SB):
        rows = slice(start, start + SB)
        one, two = amplitudes(raw, rows)
        level[rows, :] = (one * weights[rows, 0:1] + two * weights[rows, 1:2]).astype(jnp.bfloat16)

    def total(levels, chosen):
        return jnp.dot(
            levels[...], chosen.astype(jnp.bfloat16), preferred_element_type=jnp.float32
        )

    source, out_bin = (lax.broadcasted_iota(jnp.int32, (BAND, BAND), d) for d in range(2))
    sums = total(level, jnp.where(jnp.abs(source - out_bin) <= HALF, 1.0, 0.0))
    lane, edge_out = (lax.broadcasted_iota(jnp.int32, (2 * HALF, BAND), d) for d in range(2))
    for s in range(2):
        edge = lane - s * HALF
        ours = (edge >= 0) & (edge < HALF)
        below = jnp.where(ours & (edge_out <= edge), 1.0, 0.0)
        above = jnp.where(ours & (edge_out >= edge + BAND - HALF), 1.0, 0.0)
        beside = total(inside, jnp.where(odd > 0, below, above))
        beside += total(across, jnp.where(odd > 0, above, below))
        sums += beside * weights[:CH, s : s + 1]
    window[...] = sums
    for start in range(0, CH, SB):
        rows = slice(start, start + SB)
        one, two = weights[rows, 0:1], weights[rows, 1:2]
        mean = window[rows, :] / (count * jnp.maximum(one + two, 1.0))
        scale = 1.0 / (mean + EPS)
        one, two = one * scale, two * scale
        for i in range(PARTS):
            white = part(raw, rows, i) * (two if i % 2 else one)
            out[rows, i * BAND : (i + 1) * BAND] = white.astype(jnp.bfloat16)


def plain(block):
    return lambda rows, lanes=slice(None): block[rows, lanes].astype(jnp.float32)


def chosen(odd, even_block, odd_block):
    def read(rows, lanes=slice(None)):
        both = [x[rows, lanes].astype(jnp.float32) for x in (even_block, odd_block)]
        return jnp.where(odd > 0, both[1], both[0])

    return read


def rotate(read, table, out):
    for u in range(SUB):
        for s in range(2):
            lanes = [slice(i * BAND, (i + 1) * BAND) for i in (s, 2 + s)]
            real, imag = (read(slice(u * SB, (u + 1) * SB), x) for x in lanes)
            for lag in range(LAGS):
                dest = slice((u * LAGS + lag) * SB, (u * LAGS + lag + 1) * SB)
                turned = real, imag
                if lag != LAGS // 2:
                    cosine, sine = table[lag : lag + 1, :], table[4 + lag : 5 + lag, :]
                    turned = real * cosine + imag * sine, imag * cosine - real * sine
                for x, value in zip(lanes, turned):
                    out[dest, x] = value.astype(jnp.bfloat16)


def rotate_kernel(white, table, out, blank):
    rotate(plain(white), table, out)
    blank[...] = jnp.zeros_like(blank)


def place(out, odd, read):
    for u in range(SUB):
        wide = read(slice(u * SB, (u + 1) * SB))
        for target in range(N_FREQ):
            half = lax.rem(odd + target, 2)
            row = half * HALF_ROWS + (target // 2) * ROWS + u * SHARE
            out[pl.ds(pl.multiple_of(row, SHARE), SHARE), :] = wide[
                target * SHARE : (target + 1) * SHARE
            ]


def product(left, right):
    return lax.dot_general(
        left, right, (((1,), (1,)), ((), ())), preferred_element_type=jnp.float32
    )


def prepare(odd, behind, block, table, left, right_after):
    @pl.when(behind)
    def _():
        place(left, odd, plain(block))

    @pl.when(jnp.logical_not(behind))
    def _():
        rotate(plain(block), table, right_after)


def first_kernel(odd, place_of, listed, first, right_here, table, left, right_after):
    prepare(odd[0], odd[0] == 0, first, table, left, right_after)


def second_kernel(
    odd, left_in, right_in, second, right_here, table, left, right_after, mine, theirs
):
    prepare(odd[0], odd[0] != 0, second, table, left, right_after)
    rows = left[...].astype(jnp.bfloat16)
    for d, right in enumerate((right_here, right_after)):
        tile = product(rows, right[...]).astype(jnp.bfloat16)
        mine[:, d * COLS : (d + 1) * COLS] = tile[:HALF_ROWS]
        theirs[:, d * COLS : (d + 1) * COLS] = tile[HALF_ROWS:]


def gains_kernel(odd, first, here, second, theirs, out, left, right):
    def flags(read):
        return read(slice(CH, CH + 16), slice(0, WIDE))[:8]

    columns = flags(chosen(odd[0], first, second)).T
    place(left, odd[0], lambda rows: columns[rows])
    for d, read in enumerate((plain(here), chosen(odd[0], second, first))):
        valid = flags(read)
        for v in range(SUB):
            chunk = valid[:, v * SB : (v + 1) * SB]
            right[:, d * COLS + v * LAGS * SB : d * COLS + (v + 1) * LAGS * SB] = (
                jnp.concatenate([chunk] * LAGS, axis=1)
            )
    joint = jnp.dot(left[:HALF_ROWS, :], right[...], preferred_element_type=jnp.float32)
    out[...] = jnp.where(joint > 1.5, (2 * FREQS) ** -0.5, FREQS**-0.5)


def dispatch_kernel(place_of, listed, mine, other, gain, blank, out, total):
    total[...] = (mine[...].astype(jnp.float32) + other[...].astype(jnp.float32)) * gain[...]
    for slot in range(REACH * SUB * SUB):
        d, u, v = slot // (SUB * SUB), slot // SUB % SUB, slot % SUB
        keep = listed[slot].astype(jnp.float32)
        for chip in range(CHIPS):
            tile = total[
                chip * ROWS + u * SHARE : chip * ROWS + (u + 1) * SHARE,
                d * COLS + v * LAGS * SB : d * COLS + (v + 1) * LAGS * SB,
            ]
            out[place_of[slot], chip] = (tile * keep).astype(jnp.bfloat16)


def collect_kernel(received, out, sums, done):
    half = BLOCKS // 2
    copies = []
    for part_of in range(2):
        for b in range(part_of * half, (part_of + 1) * half):
            total = received[(b + 1) % BLOCKS, 0].astype(jnp.float32)
            for chip in range(1, CHIPS):
                total += received[(b + 1) % BLOCKS, chip].astype(jnp.float32)
            sums[b] = total.astype(jnp.bfloat16)
        rows = pl.ds(part_of * half, half)
        copies.append(pltpu.make_async_copy(sums.at[rows], out.at[rows], done.at[part_of]))
        copies[-1].start()
    for copy in copies:
        copy.wait()


def spread(x, forward):
    route = [
        (b * N_FREQ + k, (b + (1 if k % 2 == forward else -1)) % BLOCKS * N_FREQ + k)
        for b in range(BLOCKS)
        for k in range(N_FREQ)
    ]
    return lax.ppermute(x, ("chan", "freq"), route)


def swap(x, first):
    pairs = [(k, k + 1) for k in range(first, N_FREQ - 1, 2)]
    return lax.ppermute(x, "freq", pairs + [(k, i) for i, k in pairs])


def bf16(*shape):
    return jax.ShapeDtypeStruct(shape, jnp.bfloat16)


def kernel(fn, out_shape, inputs, scratch=(), scalars=0, mib=8, aliases=()):
    return pl.pallas_call(
        fn,
        out_shape=out_shape,
        in_specs=[SMEM] * scalars + [VMEM] * (inputs - scalars),
        out_specs=jax.tree.map(lambda _: VMEM, out_shape),
        scratch_shapes=[pltpu.VMEM(shape, dtype) for shape, dtype in scratch],
        compiler_params=pltpu.CompilerParams(vmem_limit_bytes=mib * MIB),
        input_output_aliases=dict(aliases),
        name=fn.__name__,
    )


def body(spectra, validity, pair_mask, owners):
    f32 = jnp.float32
    chan, freq = lax.axis_index("chan"), lax.axis_index("freq")
    odd = (freq % 2)[None]
    table = lax.dynamic_index_in_dim(jnp.asarray(lag_tables()), freq, 0, keepdims=False)
    raw = spectra.reshape(CH, PARTS * BAND)
    edges = bf16(CH, 2 * HALF)
    to_across = kernel(across_kernel, edges, 2, scalars=1)(odd, raw)
    across = swap(to_across, 1)
    to_inside = kernel(inside_kernel, edges, 3, scalars=1)(odd, raw, to_across)
    tail, columns = kernel(
        validity_kernel,
        (bf16(16, PARTS * BAND), jax.ShapeDtypeStruct((WIDE, 8), f32)),
        2,
        [((16, PARTS * BAND), f32)],
    )(to_inside, validity.T)
    inside = swap(to_inside, 0)
    block = bf16(CH + 16, PARTS * BAND)
    white = kernel(
        whiten_kernel, block, 7, [((CH, BAND), jnp.bfloat16), ((CH, BAND), f32)], scalars=1
    )(freq[None], raw, across, inside, tail, columns, table)
    first = spread(white, 0)
    second = spread(white, 1)
    sending = bf16(BLOCKS, CHIPS, SHARE, LAGS * SB)
    right_here, blank = kernel(rotate_kernel, (bf16(COLS, PARTS * BAND), sending), 2)(white, table)

    source = (chan + BLOCKS - 1) % BLOCKS
    listed = pair_mask[source].reshape(-1)
    place_of = owners[source]
    half = bf16(HALF_ROWS, REACH * COLS)
    kept = (
        jax.ShapeDtypeStruct((2 * HALF_ROWS, PARTS * BAND), f32),
        bf16(COLS, PARTS * BAND),
    )
    left, right_after = kernel(first_kernel, kept, 6, scalars=3)(
        odd, place_of, listed, first, right_here, table
    )
    _, _, mine, theirs = kernel(
        second_kernel, (*kept, half, half), 6, scalars=1, aliases={1: 0, 2: 1}
    )(odd, left, right_after, second, right_here, table)
    other = lax.ppermute(theirs, "freq", [(k, k ^ 1) for k in range(N_FREQ)])
    gain = kernel(
        gains_kernel,
        jax.ShapeDtypeStruct((HALF_ROWS, REACH * COLS), f32),
        5,
        [((2 * HALF_ROWS, 8), f32), ((8, REACH * COLS), f32)],
        scalars=1,
    )(odd, first, white, second, theirs)
    outgoing = kernel(
        dispatch_kernel,
        sending,
        6,
        [((HALF_ROWS, REACH * COLS), f32)],
        scalars=2,
        aliases={5: 0},
    )(place_of, listed, mine, other, gain, blank)
    groups = [
        [
            b * N_FREQ + 2 * chip + core
            for b in range(BLOCKS)
            for chip in range(CHIPS)
        ]
        for core in range(2)
    ]
    received = lax.all_to_all(
        outgoing.reshape(BLOCKS * CHIPS, SHARE, LAGS * SB),
        ("chan", "freq"),
        0,
        0,
        tiled=True,
        axis_index_groups=groups,
    )
    merged = pl.pallas_call(
        collect_kernel,
        out_shape=bf16(BLOCKS, SHARE, LAGS * SB),
        in_specs=[VMEM],
        out_specs=pl.BlockSpec(memory_space=pl.ANY),
        scratch_shapes=[
            pltpu.VMEM((BLOCKS, SHARE, LAGS * SB), jnp.bfloat16),
            pltpu.SemaphoreType.DMA((2,)),
        ],
        compiler_params=pltpu.CompilerParams(vmem_limit_bytes=4 * MIB),
        name="collect_kernel",
    )(received.reshape(BLOCKS, CHIPS, SHARE, LAGS * SB))
    return merged[None, :, None]


def solution(mesh):
    return jax.shard_map(
        body,
        mesh=mesh,
        in_specs=(P("chan", None, None, "freq"), P("chan", None), P(), P()),
        out_specs=P("chan", None, None, "freq", None),
        check_vma=False,
    )
```
